512 devices in a mesh: gx: 8 (over z), gy: 8 (over y_hi, core), af: 8 (over y_lo, x).
Axes of the slice: x: 4, y: 8 (y_hi: 4, y_lo: 2; y = y_hi * 2 + y_lo), z: 8, core: 2. Of those that a mesh axis runs over, the one named last changes fastest.
Arguments:
- volume: bfloat16 [1, 64, 64, 16, 128], P(None, 'gx', 'gy', None, 'af'), may hold values from -6 to 6
- first_filter: bfloat16 [128, 27, 128], P('af'), may hold values from -0.109375 to 0.109375
- second_filter: bfloat16 [128, 27, 128], P('af'), may hold values from -0.109375 to 0.109375
- out_grad: bfloat16 [1, 64, 64, 16, 128], P(None, 'gx', 'gy', None, 'af'), may hold values from -6 to 6
Outputs:
- output: bfloat16 [1, 64, 64, 16, 128], P(None, 'gx', 'gy', None, 'af')
- volume_grad: bfloat16 [1, 64, 64, 16, 128], P(None, 'gx', 'gy', None, 'af')
- first_grad: float32 [128, 27, 128], P('af')
- second_grad: float32 [128, 27, 128], P('af')
The draws below stay inside these ranges and needn't reach their ends.
All inputs are finite; a program needn't handle non-finite values.
Results may differ from the reference program's by a relative error of at most 0.017.
Values may be sent and summed in bfloat16 or wider, within the bound.
No kernel may reach another device: no remote copies, remote signals or barrier semaphores. Data moves between devices by JAX's collectives and lax.ppermute only.
A program may use at most 192 MiB of HBM per device.

```python
import math
import jax
import jax.numpy as jnp
from jax import lax

C = 128
BATCH = 1
NZ = 16
NX = 64
NY = 64


def levels(rng, dims, pieces, low, top_value):
    factor_of, own = 1.0, jax.random.fold_in(rng, 6)
    for dim, parts in pieces:
        draws = jnp.exp(jax.random.uniform(jax.random.fold_in(own, dim), (parts,), jnp.float32, low / len(pieces), top_value / len(pieces)))
        factor_of = factor_of * jnp.repeat(draws, dims[dim] // parts).reshape([-1 if axis == dim else 1 for axis in range(len(dims))])
    return factor_of


def scatter_about(key, dims, scale, most, pieces=(), held_as=jnp.bfloat16):
    loudness = levels(key, dims, pieces, -0.22, 0.18) if pieces else 1.0
    array = jax.random.normal(key, dims, jnp.float32) * scale * loudness
    return jnp.minimum(jnp.maximum(array, -most), most).astype(held_as)


def setup_inputs(seed: int = 0) -> dict:
    seeds = jax.random.split(jax.random.key(seed), 5)
    return {
        "volume": scatter_about(seeds[0], (BATCH, NX, NY, NZ, C), 1.0, 6.0, ((1, 8), (2, 8), (4, 8))),
        "first_filter": scatter_about(seeds[1], (C, 27, C), (27 * C) ** -0.5, 0.109375, ((0, 8),)),
        "second_filter": scatter_about(seeds[2], (C, 27, C), (27 * C) ** -0.5, 0.109375, ((0, 8),)),
        "out_grad": scatter_about(seeds[3], (BATCH, NX, NY, NZ, C), 1.0, 6.0, ((1, 8), (2, 8), (4, 8))),
    }


def conv_same(field, weight):
    w5 = weight.astype(jnp.float32).reshape(weight.shape[0], 3, 3, 3, weight.shape[2])
    return lax.conv_general_dilated(field.astype(jnp.float32), w5, (1, 1, 1), 'SAME', dimension_numbers=('NDHWC', 'ODHWI', 'NDHWC'), precision=lax.Precision.HIGHEST)

def conv_back(grad, weight):
    w5 = weight.astype(jnp.float32).reshape(weight.shape[0], 3, 3, 3, weight.shape[2])
    w5 = w5[:, ::-1, ::-1, ::-1, :]
    return lax.conv_general_dilated(grad.astype(jnp.float32), w5, (1, 1, 1), 'SAME', dimension_numbers=('NDHWC', 'IDHWO', 'NDHWC'), precision=lax.Precision.HIGHEST)

def filter_grad(field, grad):
    padded = jnp.pad(field.astype(jnp.float32), ((0, 0), (1, 1), (1, 1), (1, 1), (0, 0)))
    gradf = grad.astype(jnp.float32)
    sx, sy, sz = (grad.shape[1], grad.shape[2], grad.shape[3])
    taps = []
    for first in range(3):
        for second in range(3):
            for third in range(3):
                piece = padded[:, first:first + sx, second:second + sy, third:third + sz, :]
                taps.append(jnp.einsum('bxyzi,bxyzo->oi', piece, gradf, precision=lax.Precision.HIGHEST))
    count = grad.shape[0] * sx * sy * sz
    return jnp.stack(taps, axis=1) * (1.0 / math.sqrt(count))

def reference(volume, first_filter, second_filter, out_grad):
    pre = conv_same(volume, first_filter).astype(jnp.bfloat16)
    pref = pre.astype(jnp.float32)
    hidden = jax.nn.silu(pref).astype(jnp.bfloat16)
    output = conv_same(hidden, second_filter).astype(jnp.bfloat16)
    second_grad = filter_grad(hidden, out_grad)
    hidden_grad = conv_back(out_grad, second_filter)
    sig = jax.nn.sigmoid(pref)
    pre_grad = (hidden_grad * sig * (1.0 + pref * (1.0 - sig))).astype(jnp.bfloat16)
    volume_grad = conv_back(pre_grad, first_filter).astype(jnp.bfloat16)
    first_grad = filter_grad(volume, pre_grad)
    return (output, volume_grad, first_grad, second_grad)
```

```python
import functools
import math

import jax
import jax.numpy as jnp
from jax import lax
from jax.experimental import pallas as pl
from jax.experimental.pallas import tpu as pltpu
from jax.sharding import PartitionSpec as P

BF = jnp.bfloat16
F32 = jnp.float32
T = 128
VMEM = pl.BlockSpec(memory_space=pltpu.VMEM)
SMEM = pl.BlockSpec(memory_space=pltpu.SMEM)
GY = ("yh", "co")
EXT = 25 * T
MID = 21 * T
OWN = 17 * T


def call(kernel, outs, scratch=(), scalars=False):
    def run(*args):
        return pl.pallas_call(
            kernel,
            out_shape=outs,
            in_specs=[SMEM if scalars and k == 0 else VMEM for k in range(len(args))],
            scratch_shapes=scratch,
            compiler_params=pltpu.CompilerParams(vmem_limit_bytes=48 << 20),
        )(*args)

    return run


def lanes(rows=16):
    return lax.broadcasted_iota(jnp.int32, (rows, T), 1)


def rolled(x, shift):
    size = x.shape[1]
    return pltpu.roll(x, shift % size, 1) if shift % size else x


def regroup(tiles):
    lane = lanes()
    tiles = list(tiles)
    for bit in (1, 2, 4):
        clear = (lane // (16 * bit)) % 2 == 0
        for u in range(8):
            if u & bit:
                continue
            first, second = tiles[u], tiles[u + bit]
            tiles[u] = jnp.where(clear, first, rolled(second, 16 * bit))
            tiles[u + bit] = jnp.where(clear, rolled(first, -16 * bit), second)
    return tiles


def pack_kernel(vol_hbm, grad_hbm, w1_hbm, w2_hbm, send, w1, w2, vol, grad, sems):
    copies = [
        pltpu.make_async_copy(source, target, sems.at[k])
        for k, (source, target) in enumerate(((vol_hbm, vol), (grad_hbm, grad), (w1_hbm, w1), (w2_hbm, w2)))
    ]
    for copy in copies:
        copy.start()
    for a, ref in enumerate((vol, grad)):
        copies[a].wait()
        for x in range(8):
            tile = ref[0, x].reshape(T, 16).astype(F32).T.astype(BF)
            for j in range(8):
                send[j, a * 8 + x] = tile
    for f, ref in enumerate((w1, w2)):
        copies[2 + f].wait()
        for m in range(4):
            tiles = [ref[8 * m + u].astype(F32) if 8 * m + u < 27 else jnp.zeros((16, T), F32) for u in range(8)]
            for j, tile in enumerate(regroup(tiles)):
                send[j, 16 + 4 * f + m] = tile.astype(BF)


def gathered(ref, k):
    return ref[:, k].reshape(T, T)


def face_kernel(block, low, high):
    for a in range(2):
        for p in range(2):
            low[2 * a + p] = gathered(block, 8 * a + p)
            high[2 * a + p] = gathered(block, 8 * a + 6 + p)


def edge_kernel(block, before, after, low, high):
    group = lanes(T) // 32
    for a in range(2):
        lows, highs = [None] * 3, [None] * 3
        for r in range(12):
            if r < 2:
                row = before[2 * a + r]
            elif r < 10:
                row = gathered(block, 8 * a + r - 2)
            else:
                row = after[2 * a + r - 10]
            row = row.astype(F32)
            for tiles, slot, off in ((lows, (r + 1) % 12, 0), (highs, r, 3)):
                q, k = slot // 4, slot % 4
                moved = rolled(row, 32 * k)
                tiles[q] = moved if tiles[q] is None else jnp.where(group == (k + off) % 4, moved, tiles[q])
        for q in range(3):
            low[a, q] = lows[q].astype(BF)
            high[a, q] = highs[q].astype(BF)


def product(left, right, out, width):
    for n in range(0, width, 640):
        size = min(640, width - n)
        out[:, n : n + size] = jnp.dot(left, right[:, n : n + size], preferred_element_type=F32)


def combine(prods, sign, width):
    depth = lax.broadcasted_iota(jnp.int32, (16, width), 1) % 16
    total = None
    for e in range(3):
        part = None
        for c in range(3):
            term = None
            for a in range(3):
                t = 9 * a + 3 * c + e
                start = 256 * a if sign > 0 else 256 * (2 - a)
                piece = prods[t * 16 : t * 16 + 16, start : start + width]
                term = piece if term is None else term + piece
            term = rolled(term, -sign * (c - 1) * 16)
            part = term if part is None else part + term
        step = sign * (e - 1)
        if step:
            part = rolled(part, -step)
            part = jnp.where(depth != (15 if step > 0 else 0), part, 0.0)
        total = part if total is None else total + part
    return total


def shifted(field, sign, out):
    depth = lax.broadcasted_iota(jnp.int32, (16, OWN), 1) % 16
    for c in range(3):
        moved = rolled(field, sign * (c - 1) * 16)
        for e in range(3):
            step = sign * (e - 1)
            piece = rolled(moved, step)
            if step:
                piece = jnp.where(depth != (0 if step > 0 else 15), piece, 0.0)
            k = (c * 3 + e) * 16
            out[k : k + 16, :] = piece.astype(BF)


def correlate(shifts, field, sign, out):
    for a in range(3):
        start = 2 * T + 256 * (a if sign > 0 else 2 - a)
        out[a * 144 : a * 144 + 144, :] = lax.dot_general(
            shifts[...],
            field[:, start : start + OWN],
            (((1,), (1,)), ((), ())),
            preferred_element_type=F32,
        )


def gathered_filter(ref, first):
    parts = [gathered(ref, first + m).astype(F32).T.astype(BF) for m in range(4)]
    return jnp.concatenate(parts, axis=0)[0:432]


def first_kernel(place, block, before, after, ybefore, yafter, w1rows, send, keep_out, give_out, vol, grad, prods1, prods2, shifts, sums, halves):
    for a, ref in enumerate((vol, grad)):
        def put(tile, value):
            ref[:, tile * T : tile * T + T] = value

        for r in range(12):
            if r < 2:
                value = before[2 * a + r]
            elif r < 10:
                value = gathered(block, 8 * a + r - 2)
            else:
                value = after[2 * a + r - 10]
            put(2 * r + 1, value)
        for q in range(3):
            late, early = yafter[a, q].astype(F32), ybefore[a, q].astype(F32)
            for k in range(4):
                value = rolled(jnp.where(lanes(T) // 32 == k, late, early), -32 * k).astype(BF)
                put(2 * (4 * q + k), value)
                if q + k == 0:
                    put(2 * 12, value)
    product(w1rows[...].reshape(432, T), vol, prods1, EXT)
    product(gathered_filter(block, 20), grad, prods2, EXT)

    lane = lax.broadcasted_iota(jnp.int32, (16, MID), 1)
    tile = lane // T
    low_x, high_x = place[0] == 0, place[0] == 7
    low_y, high_y = place[1] == 0, place[1] == 7
    halo = tile % 2 == 0
    early = halo & (lane % T >= 64)
    late = halo & (lane % T < 64)
    row = jnp.where(early, tile // 2 + 1, tile // 2 + jnp.where(halo, 0, 1))
    bad = (row <= 1) & low_x
    bad = bad | ((row >= 10) & high_x)
    bad = bad | (early & low_y) | (late & high_y)
    keep = jnp.logical_not(bad)

    pre = combine(prods1, 1, MID).astype(BF).astype(F32)
    sig = jax.nn.sigmoid(pre)
    hidden = jnp.where(keep, pre * sig, 0.0).astype(BF).astype(F32)
    back = combine(prods2, -1, MID)
    back = jnp.where(keep, back * sig * (1.0 + pre * (1.0 - sig)), 0.0).astype(BF).astype(F32)

    narrow = lanes()
    for a, field in enumerate((hidden, back)):
        for r in range(10):
            tile_r = field[:, (2 * r + 1) * T : (2 * r + 2) * T].astype(BF)
            for j in range(8):
                send[j, a * 13 + r] = tile_r
        for q in range(3):
            packed = jnp.zeros((16, T), F32)
            for k in range(4):
                h = 4 * q + k
                if h > 10:
                    continue
                here = ((narrow + 16) % T) // 32 == k
                packed = jnp.where(here, rolled(field[:, 2 * h * T : 2 * h * T + T], 32 * k), packed)
            packed = packed.astype(BF)
            for j in range(8):
                send[j, a * 13 + 10 + q] = packed

    mine = lax.broadcasted_iota(jnp.int32, (16, OWN), 1) // T % 2 == 1
    shifted(jnp.where(mine, back[:, 2 * T : 2 * T + OWN], 0.0), 1, shifts)
    correlate(shifts, vol, 1, sums)
    for n in range(32):
        for h in range(2):
            value = sums[n * 16 + 8 * h : n * 16 + 8 * h + 8, :] if n < 27 else jnp.zeros((8, T), F32)
            halves[h, n, 0:8, :] = value
    shifted(jnp.where(mine, hidden[:, 2 * T : 2 * T + OWN], 0.0), -1, shifts)
    correlate(shifts, grad, -1, sums)
    sums[432:512, :] = jnp.zeros((80, T), F32)
    for m in range(4):
        block = sums[T * m : T * m + T, :].T
        for k in range(8):
            for h in range(2):
                row = 16 * k + 8 * h
                halves[h, 4 * k + m, 8:16, :] = block[row : row + 8]
    keep_out[...] = halves[place[2]]
    give_out[...] = halves[1 - place[2]]


def second_kernel(block, middle, w2rows, out, vgrad, hid, pre, prods):
    for a, ref in enumerate((hid, pre)):
        for r in range(10):
            ref[:, (2 * r + 1) * T : (2 * r + 2) * T] = gathered(middle, a * 13 + r)
        for h in range(11):
            value = gathered(middle, a * 13 + 10 + h // 4)
            if h % 4:
                value = rolled(value.astype(F32), -32 * (h % 4)).astype(BF)
            ref[:, 2 * h * T : 2 * h * T + T] = value

    def store(ref, value):
        for x in range(8):
            tile = value[:, (2 * x + 1) * T : (2 * x + 2) * T]
            ref[0, x] = tile.T.astype(BF).reshape(8, 16, 16)

    product(w2rows[...].reshape(432, T), hid, prods, MID)
    store(out, combine(prods, 1, OWN))
    product(gathered_filter(block, 16), pre, prods, MID)
    store(vgrad, combine(prods, -1, OWN))


def pair_kernel(mine, other, out):
    out[...] = mine[...] + other[...]


def sum_kernel(factor, parts, out):
    total = parts[0]
    for k in range(1, 32):
        total = total + parts[k]
    out[...] = total * factor


def merge_kernel(place, mine, other, first, second):
    mine, other = mine[...], other[...]
    even = place[2] == 0
    low, high = jnp.where(even, mine, other), jnp.where(even, other, mine)
    first[...] = jnp.concatenate([low[0:8], high[0:8]], axis=0).astype(BF)
    second[...] = jnp.concatenate([low[8:16], high[8:16]], axis=0).astype(BF)


def spread_kernel(first, second, out):
    for j in range(32):
        out[j, 0:16, :] = first[...]
        out[j, 16:32, :] = second[...]


def last_kernel(parts, first, second):
    for t in range(27):
        first[t] = parts[t, 0:16, :].astype(F32)
    for m in range(4):
        tiles = regroup([parts[4 * k + m, 16:32, :].astype(F32) for k in range(8)])
        for u in range(8):
            if 8 * m + u < 27:
                second[8 * m + u] = tiles[u]


def shape(*dims, dtype=BF):
    return jax.ShapeDtypeStruct(dims, dtype)


def neighbours(low, high, axis):
    size = lax.axis_size(axis)
    up = [(i, i + 1) for i in range(size - 1)]
    before = lax.ppermute(high, axis, up)
    after = lax.ppermute(low, axis, [(j, i) for i, j in up])
    return before, after


def on_device(volume, first_filter, second_filter, out_grad):
    factor = 1.0 / math.sqrt(64 * 64 * 16)
    place = jnp.stack([lax.axis_index("gx"), lax.axis_index(GY), lax.axis_index("co")]).astype(jnp.int32)
    w1 = first_filter.transpose(1, 0, 2)
    w2 = second_filter.transpose(1, 0, 2)
    filters = shape(27, 16, T)
    send, w1, w2 = pl.pallas_call(
        pack_kernel,
        out_shape=(shape(8, 24, 16, T), filters, filters),
        in_specs=[pl.BlockSpec(memory_space=pltpu.HBM)] * 4,
        scratch_shapes=[pltpu.VMEM((1, 8, 8, 16, 16), BF)] * 2 + [pltpu.SemaphoreType.DMA((4,))],
    )(volume, out_grad, w1, w2)
    block = lax.all_to_all(send, "af", 0, 0)
    face = shape(4, T, T)
    low, high = call(face_kernel, (face, face))(block)
    before, after = neighbours(low, high, "gx")
    edge = shape(2, 3, T, T)
    low, high = call(edge_kernel, (edge, edge))(block, before, after)
    ybefore, yafter = neighbours(low, high, GY)
    middle, keep, give = call(
        first_kernel,
        (shape(8, 26, 16, T), shape(32, 16, T, dtype=F32), shape(32, 16, T, dtype=F32)),
        [
            pltpu.VMEM((T, EXT), BF),
            pltpu.VMEM((T, EXT), BF),
            pltpu.VMEM((432, EXT), F32),
            pltpu.VMEM((432, EXT), F32),
            pltpu.VMEM((144, OWN), BF),
            pltpu.VMEM((512, T), F32),
            pltpu.VMEM((2, 32, 16, T), F32),
        ],
        scalars=True,
    )(place, block, before, after, ybefore, yafter, w1)
    swap = [(0, 1), (1, 0)]
    other = lax.ppermute(give, "co", swap)
    parts = call(pair_kernel, shape(32, 16, T, dtype=F32))(keep, other)
    parts = lax.all_to_all(parts, ("gx", "yh"), 0, 0)
    parts, middle = lax.optimization_barrier((parts, middle))
    middle = lax.all_to_all(middle, "af", 0, 0)
    part = call(functools.partial(sum_kernel, factor), shape(16, T, dtype=F32))(parts)
    other = lax.ppermute(part, "co", swap)
    first, second = call(merge_kernel, (shape(16, T), shape(16, T)), scalars=True)(place, part, other)
    second = lax.ppermute(second, ("gx", "af"), [(a * 8 + k, k * 8 + a) for a in range(8) for k in range(8)])
    first, second, middle = lax.optimization_barrier((first, second, middle))
    parts = call(spread_kernel, shape(32, 32, T))(first, second)
    parts = lax.all_to_all(parts, ("gx", "yh"), 0, 0)
    output, volume_grad = call(
        second_kernel,
        (shape(1, 8, 8, 16, 16), shape(1, 8, 8, 16, 16)),
        [pltpu.VMEM((T, MID), BF), pltpu.VMEM((T, MID), BF), pltpu.VMEM((432, MID), F32)],
    )(block, middle, w2)
    wide = shape(27, 16, T, dtype=F32)
    first_grad, second_grad = call(last_kernel, (wide, wide))(parts)
    return output, volume_grad, first_grad.transpose(1, 0, 2), second_grad.transpose(1, 0, 2)


def solution(mesh):
    split = jax.sharding.Mesh(mesh.devices.reshape(8, 4, 2, 8), ("gx", "yh", "co", "af"))
    cells = P(None, "gx", GY, None, "af")
    weights = P("af", None, None)
    return jax.shard_map(
        on_device,
        mesh=split,
        in_specs=(cells, weights, weights, cells),
        out_specs=(cells, cells, weights, weights),
        check_vma=False,
    )
```

```python
import functools
import math

import jax
import jax.numpy as jnp
from jax import lax
from jax.experimental import pallas as pl
from jax.experimental.pallas import tpu as pltpu
from jax.sharding import PartitionSpec as P

BF = jnp.bfloat16
F32 = jnp.float32
T = 128
VMEM = pl.BlockSpec(memory_space=pltpu.VMEM)
SMEM = pl.BlockSpec(memory_space=pltpu.SMEM)
HBM = pl.BlockSpec(memory_space=pltpu.HBM)
GY = ("yh", "co")
EXT = 25 * T
MID = 21 * T
OWN = 17 * T


def call(kernel, outs, scratch=(), scalars=False, hbm=False, limit=8):
    def run(*args):
        return pl.pallas_call(
            kernel,
            out_shape=outs,
            in_specs=[HBM if hbm else SMEM if scalars and k == 0 else VMEM for k in range(len(args))],
            scratch_shapes=scratch,
            compiler_params=pltpu.CompilerParams(vmem_limit_bytes=limit << 20),
        )(*args)

    return run


def lanes(rows=16):
    return lax.broadcasted_iota(jnp.int32, (rows, T), 1)


def rolled(x, shift):
    size = x.shape[1]
    return pltpu.roll(x, shift % size, 1) if shift % size else x


def regroup(tiles):
    lane = lanes()
    tiles = list(tiles)
    for bit in (1, 2, 4):
        clear = (lane // (16 * bit)) % 2 == 0
        for u in range(8):
            if u & bit:
                continue
            first, second = tiles[u], tiles[u + bit]
            tiles[u] = jnp.where(clear, first, rolled(second, 16 * bit))
            tiles[u + bit] = jnp.where(clear, rolled(first, -16 * bit), second)
    return tiles


def pack_kernel(vol_hbm, grad_hbm, own, low, vol, grad, sems):
    copies = [
        pltpu.make_async_copy(source, target, sems.at[k])
        for k, (source, target) in enumerate(((vol_hbm, vol), (grad_hbm, grad)))
    ]
    for copy in copies:
        copy.start()
    for a, ref in enumerate((vol, grad)):
        copies[a].wait()
        for x in range(8):
            tile = ref[0, x].reshape(T, 16).astype(F32).T.astype(BF)
            own[a, x] = tile
            if x < 4:
                low[a, x] = tile


def weight_kernel(w1_hbm, w2_hbm, out, w1, w2, sems):
    copies = [
        pltpu.make_async_copy(source, target, sems.at[k])
        for k, (source, target) in enumerate(((w1_hbm, w1), (w2_hbm, w2)))
    ]
    for copy in copies:
        copy.start()
    for f, ref in enumerate((w1, w2)):
        copies[f].wait()
        for m in range(4):
            tiles = [ref[8 * m + u].astype(F32) if 8 * m + u < 27 else jnp.zeros((16, T), F32) for u in range(8)]
            for j, tile in enumerate(regroup(tiles)):
                out[j, 4 * f + m] = tile.astype(BF)


def gathered(ref, k):
    return ref[:, k].reshape(T, T)


def row_of(own, nextx, a, r):
    return (own[a, r] if r < 8 else nextx[a, r - 8]).astype(F32)


def edge_kernel(own, nextx, out):
    first = lanes() < 64
    for a in range(2):
        for p in range(6):
            odd = rolled(row_of(own, nextx, a, 2 * p + 1), 64)
            out[a, p] = jnp.where(first, row_of(own, nextx, a, 2 * p), odd).astype(BF)


def send_kernel(own, nextx, nexty, weights, send, mine):
    lane = lanes()
    for a in range(2):
        rows = [row_of(own, nextx, a, r) for r in range(12)]
        nexts = []
        for r in range(12):
            tile = nexty[a, r // 2].astype(F32)
            nexts.append(rolled(tile, 64) if r % 2 else tile)
        tiles = [rolled(jnp.where(lane < 32, nexts[r], rows[r]), -32).astype(BF) for r in range(12)]
        packed = [None] * 6
        for h in range(13):
            q, k = h % 12 // 2, h % 2
            if h < 12:
                moved = rolled(rows[h], 64 * k - 32)
                here = lane // 32 == (3 if k == 0 else 1)
                packed[q] = moved if packed[q] is None else jnp.where(here, moved, packed[q])
            if h > 0:
                moved = rolled(nexts[h - 1], 64 * k - 32)
                here = lane // 32 == 2 * k
                packed[q] = moved if packed[q] is None else jnp.where(here, moved, packed[q])
        tiles += [tile.astype(BF) for tile in packed]
        for k, tile in enumerate(tiles):
            if a == 1 and 2 <= k < 10:
                mine[k - 2] = tile
            for j in range(8):
                send[j, a * 18 + k] = tile
    for k in range(8):
        for j in range(8):
            send[j, 36 + k] = weights[j, k]


def product(left, right, out, width):
    for n in range(0, width, 640):
        size = min(640, width - n)
        out[:, n : n + size] = jnp.dot(left, right[:, n : n + size], preferred_element_type=F32)


def cells(width, first):
    lane = lax.broadcasted_iota(jnp.int32, (16, width), 1)
    tile = lane // T + first
    own = tile % 2 == 1
    inner = lane % T
    row = jnp.where(own, tile // 2, jnp.where(inner < 64, tile // 2 - 1, tile // 2))
    column = jnp.where(own, inner // 16 + 2, jnp.where(inner < 64, inner // 16 + 10, inner // 16 - 6))
    return row, column, lane % 16


def combine(prods, sign, width, first, place):
    row, column, depth = cells(width, first)
    split_x, split_y = place[0] == 7, place[1] == 7
    inside = {
        1: jnp.where((row == 7) & split_x, 0.0, 1.0),
        -1: jnp.where((row == 8) & split_x, 0.0, 1.0),
    }
    apart = {1: (column == 7) & split_y, -1: (column == 8) & split_y}
    total = None
    for e in range(3):
        part = None
        for c in range(3):
            term = None
            for a in range(3):
                t = 9 * a + 3 * c + e
                start = 256 * a if sign > 0 else 256 * (2 - a)
                piece = prods[t * 16 : t * 16 + 16, start : start + width]
                if a != 1:
                    piece = piece * inside[sign * (a - 1)]
                term = piece if term is None else term + piece
            step = sign * (c - 1)
            if step:
                term = jnp.where(apart[step], 0.0, rolled(term, -step * 16))
            part = term if part is None else part + term
        step = sign * (e - 1)
        if step:
            part = rolled(part, -step)
            part = jnp.where(depth != (15 if step > 0 else 0), part, 0.0)
        total = part if total is None else total + part
    return total


def shifted(field, place, out):
    row, column, depth = cells(OWN, 4)
    split_x, split_y = place[0] == 7, place[1] == 7
    keep = {
        0: jnp.where((row == 8) & split_x, 0.0, 1.0).astype(BF),
        2: jnp.where((row == 7) & split_x, 0.0, 1.0).astype(BF),
    }
    for c in range(3):
        moved = rolled(field, (c - 1) * 16)
        if c != 1:
            moved = jnp.where((column == (8 if c == 2 else 7)) & split_y, 0.0, moved)
        for e in range(3):
            piece = rolled(moved, e - 1)
            if e != 1:
                piece = jnp.where(depth != (0 if e == 2 else 15), piece, 0.0)
            k = (c * 3 + e) * 16
            piece = piece.astype(BF)
            for a in range(3):
                out[a, k : k + 16, :] = piece if a == 1 else piece * keep[a]


def correlate(shifts, field, base, out):
    for a in range(3):
        start = base + 256 * a
        out[a * 144 : a * 144 + 144, :] = lax.dot_general(
            shifts[a],
            field[:, start : start + OWN],
            (((1,), (1,)), ((), ())),
            preferred_element_type=F32,
        )


def gathered_filter(ref, first):
    parts = [gathered(ref, first + m).astype(F32).T.astype(BF) for m in range(4)]
    return jnp.concatenate(parts, axis=0)[0:432]


def first_kernel(place, block, w1rows, send, sums, vol, grad, prods1, prods2, shifts):
    for a, ref in enumerate((vol, grad)):
        def put(tile, value):
            ref[:, tile * T : tile * T + T] = value

        for r in range(12):
            put(2 * r + 1, gathered(block, a * 18 + r))
        for q in range(6):
            packed = gathered(block, a * 18 + 12 + q)
            for k in range(2):
                value = rolled(packed.astype(F32), -64).astype(BF) if k else packed
                put(2 * (2 * q + k), value)
                if q + k == 0:
                    put(2 * 12, value)
    product(w1rows[...].reshape(432, T), vol, prods1, EXT)
    product(gathered_filter(block, 40), grad, prods2, EXT)

    pre = combine(prods1, 1, MID, 2, place).astype(BF).astype(F32)
    sig = jax.nn.sigmoid(pre)
    hidden = (pre * sig).astype(BF).astype(F32)
    back = combine(prods2, -1, MID, 2, place)
    back = (back * sig * (1.0 + pre * (1.0 - sig))).astype(BF).astype(F32)

    narrow = lanes()
    for a, field in enumerate((hidden, back)):
        for r in range(10):
            tile_r = field[:, (2 * r + 1) * T : (2 * r + 2) * T].astype(BF)
            for j in range(8):
                send[j, a * 13 + r] = tile_r
        for q in range(3):
            packed = jnp.zeros((16, T), F32)
            for k in range(4):
                h = 4 * q + k
                if h > 10:
                    continue
                here = ((narrow + 16) % T) // 32 == k
                packed = jnp.where(here, rolled(field[:, 2 * h * T : 2 * h * T + T], 32 * k), packed)
            packed = packed.astype(BF)
            for j in range(8):
                send[j, a * 13 + 10 + q] = packed

    mine = lax.broadcasted_iota(jnp.int32, (16, OWN), 1) // T % 2 == 1
    shifted(jnp.where(mine, back[:, 2 * T : 2 * T + OWN], 0.0), place, shifts)
    correlate(shifts, vol, 2 * T, sums)


def spread(middle, a, ref):
    for r in range(10):
        ref[:, (2 * r + 1) * T : (2 * r + 2) * T] = gathered(middle, a * 13 + r)
    for h in range(11):
        value = gathered(middle, a * 13 + 10 + h // 4)
        if h % 4:
            value = rolled(value.astype(F32), -32 * (h % 4)).astype(BF)
        ref[:, 2 * h * T : 2 * h * T + T] = value


def grad_kernel(place, own, middle, sums1, hid, send, field, shifts, sums2):
    spread(middle, 0, hid)
    field[...] = jnp.zeros((16, OWN), F32)
    for x in range(8):
        field[:, (2 * x + 1) * T : (2 * x + 2) * T] = own[x].astype(F32)
    shifted(field[...], place, shifts)
    correlate(shifts, hid, 0, sums2)
    rows = jnp.concatenate([sums1[...], sums2[...], jnp.zeros((32, T), F32)], axis=0)
    send[...] = rows.astype(BF).reshape(8, 112, T)


def second_kernel(place, block, middle, hid, w2rows, keep, give, pre, prods):
    spread(middle, 1, pre)

    def store(which, value):
        for x in range(8):
            tile = value[:, (2 * x + 1) * T : (2 * x + 2) * T].astype(BF)
            if x < 6:
                keep[which, x] = tile
            else:
                give[which, x - 6] = tile

    product(w2rows[...].reshape(432, T), hid, prods, MID)
    store(0, combine(prods, 1, OWN, 4, place))
    product(gathered_filter(block, 36), pre, prods, MID)
    store(1, combine(prods, -1, OWN, 4, place))


def back_kernel(keep, taken, rows, give):
    lane = lanes()
    for a in range(2):
        tiles = [taken[a, 0], taken[a, 1]] + [keep[a, x] for x in range(6)]
        for x, tile in enumerate(tiles):
            rows[a, x] = tile
        for q in range(2):
            packed = tiles[4 * q + 3].astype(F32)
            for k in range(3):
                moved = rolled(tiles[4 * q + k].astype(F32), 32 * k + 32)
                packed = jnp.where(lane // 32 == k, moved, packed)
            give[a, q] = packed.astype(BF)


def out_kernel(rows, taken, out, vgrad):
    lane = lanes()
    for a, ref in enumerate((out, vgrad)):
        for x in range(8):
            first = rolled(taken[a, x // 4].astype(F32), -32 * (x % 4))
            tile = jnp.where(lane < 32, first, rolled(rows[a, x].astype(F32), 32))
            ref[0, x] = tile.T.astype(BF).reshape(8, 16, 16)


def sum_kernel(factor, copies, parts, out):
    total = parts[0].astype(F32)
    for k in range(1, parts.shape[0]):
        total = total + parts[k].astype(F32)
    total = total * factor
    if copies == 1:
        out[...] = total
    for j in range(copies if copies > 1 else 0):
        out[j] = total.astype(BF)


def pair_kernel(mine, other, out):
    total = (mine[...] + other[...]).astype(BF)
    for j in range(4):
        out[j] = total


def last_kernel(parts, first, second):
    rows = parts[...].reshape(896, T).astype(F32)
    first[...] = rows[0:432].reshape(27, 16, T)
    second[...] = rows[432:864].reshape(27, 16, T)


def shape(*dims, dtype=BF):
    return jax.ShapeDtypeStruct(dims, dtype)


def cyclic(x, axis, step):
    size = lax.axis_size(axis)
    return lax.ppermute(x, axis, [(i, (i + step) % size) for i in range(size)])


def on_device(volume, first_filter, second_filter, out_grad):
    factor = 1.0 / math.sqrt(64 * 64 * 16)
    place = jnp.stack([lax.axis_index("gx"), lax.axis_index(GY)]).astype(jnp.int32)
    w1 = first_filter.transpose(1, 0, 2)
    w2 = second_filter.transpose(1, 0, 2)
    two = shape(2, 8, 16, T)
    own, low = call(
        pack_kernel,
        (two, shape(2, 4, 16, T)),
        [pltpu.VMEM((1, 8, 8, 16, 16), BF)] * 2 + [pltpu.SemaphoreType.DMA((2,))],
        hbm=True,
    )(volume, out_grad)
    nextx = cyclic(low, "gx", -1)
    nexty = cyclic(call(edge_kernel, shape(2, 6, 16, T))(own, nextx), GY, -1)
    pieces = call(
        weight_kernel,
        shape(8, 8, 16, T),
        [pltpu.VMEM((27, 16, T), BF)] * 2 + [pltpu.SemaphoreType.DMA((2,))],
        hbm=True,
    )(w1, w2)
    send, mine = call(send_kernel, (shape(8, 44, 16, T), shape(8, 16, T)))(own, nextx, nexty, pieces)
    block = lax.all_to_all(send, "af", 0, 0)
    middle, sums = call(
        first_kernel,
        (shape(8, 26, 16, T), shape(432, T, dtype=F32)),
        [
            pltpu.VMEM((T, EXT), BF),
            pltpu.VMEM((T, EXT), BF),
            pltpu.VMEM((432, EXT), F32),
            pltpu.VMEM((432, EXT), F32),
            pltpu.VMEM((3, 144, OWN), BF),
        ],
        scalars=True,
        limit=28,
    )(place, block, w1)
    middle = lax.all_to_all(middle, "af", 0, 0)
    many = shape(8, 112, T)
    hid, parts = call(
        grad_kernel,
        (shape(T, MID), many),
        [pltpu.VMEM((16, OWN), F32), pltpu.VMEM((3, 144, OWN), BF), pltpu.VMEM((432, T), F32)],
        scalars=True,
        limit=16,
    )(place, mine, middle, sums)
    keep, give = call(
        second_kernel,
        (shape(2, 6, 16, T), shape(2, 2, 16, T)),
        [pltpu.VMEM((T, MID), BF), pltpu.VMEM((432, MID), F32)],
        scalars=True,
        limit=20,
    )(place, block, middle, hid, w2)
    parts = lax.all_to_all(parts, "gx", 0, 0)
    parts, keep, give = lax.optimization_barrier((parts, keep, give))
    part = call(functools.partial(sum_kernel, 1.0, 1), shape(112, T, dtype=F32))(parts)
    other = lax.ppermute(part, "co", [(0, 1), (1, 0)])
    parts = call(pair_kernel, shape(4, 112, T))(part, other)
    rows, give = call(back_kernel, (two, shape(2, 2, 16, T)))(keep, cyclic(give, "gx", 1))
    parts = lax.all_to_all(parts, "yh", 0, 0)
    parts, rows, give = lax.optimization_barrier((parts, rows, give))
    parts = call(functools.partial(sum_kernel, factor, 8), many)(parts)
    output, volume_grad = call(out_kernel, (shape(1, 8, 8, 16, 16), shape(1, 8, 8, 16, 16)))(rows, cyclic(give, GY, 1))
    parts = lax.all_to_all(parts, "gx", 0, 0)
    wide = shape(27, 16, T, dtype=F32)
    first_grad, second_grad = call(last_kernel, (wide, wide))(parts)
    return output, volume_grad, first_grad.transpose(1, 0, 2), second_grad.transpose(1, 0, 2)


def solution(mesh):
    split = jax.sharding.Mesh(mesh.devices.reshape(8, 4, 2, 8), ("gx", "yh", "co", "af"))
    cells = P(None, "gx", GY, None, "af")
    weights = P("af", None, None)
    return jax.shard_map(
        on_device,
        mesh=split,
        in_specs=(cells, weights, weights, cells),
        out_specs=(cells, cells, weights, weights),
        check_vma=False,
    )
```

```python
import functools
import math

import jax
import jax.numpy as jnp
from jax import lax
from jax.experimental import pallas as pl
from jax.experimental.pallas import tpu as pltpu
from jax.sharding import PartitionSpec as P

BF = jnp.bfloat16
F32 = jnp.float32
T = 128
VMEM = pl.BlockSpec(memory_space=pltpu.VMEM)
SMEM = pl.BlockSpec(memory_space=pltpu.SMEM)
HBM = pl.BlockSpec(memory_space=pltpu.HBM)
GY = ("yh", "co")
EXT = 24 * T
MID = 20 * T
OWN = 16 * T


def call(kernel, outs, scratch=(), scalars=False, hbm=False, limit=8):
    def run(*args):
        return pl.pallas_call(
            kernel,
            out_shape=outs,
            in_specs=[HBM if hbm else SMEM if scalars and k == 0 else VMEM for k in range(len(args))],
            scratch_shapes=scratch,
            compiler_params=pltpu.CompilerParams(vmem_limit_bytes=limit << 20),
        )(*args)

    return run


def lanes(rows=16):
    return lax.broadcasted_iota(jnp.int32, (rows, T), 1)


def rolled(x, shift):
    size = x.shape[1]
    return pltpu.roll(x, shift % size, 1) if shift % size else x


def regroup(tiles):
    lane = lanes()
    tiles = list(tiles)
    for bit in (1, 2, 4):
        clear = (lane // (16 * bit)) % 2 == 0
        for u in range(8):
            if u & bit:
                continue
            first, second = tiles[u], tiles[u + bit]
            tiles[u] = jnp.where(clear, first, rolled(second, 16 * bit))
            tiles[u + bit] = jnp.where(clear, rolled(first, -16 * bit), second)
    return tiles


def pack_kernel(vol_hbm, grad_hbm, own, low, vol, grad, sems):
    copies = [
        pltpu.make_async_copy(source, target, sems.at[k])
        for k, (source, target) in enumerate(((vol_hbm, vol), (grad_hbm, grad)))
    ]
    for copy in copies:
        copy.start()
    for a, ref in enumerate((vol, grad)):
        copies[a].wait()
        for x in range(8):
            tile = ref[0, x].reshape(T, 16).astype(F32).T.astype(BF)
            own[a, x] = tile
            if x < 4:
                low[a, x] = tile


def weight_kernel(w1_hbm, w2_hbm, out, w1, w2, sems):
    copies = [
        pltpu.make_async_copy(source, target, sems.at[k])
        for k, (source, target) in enumerate(((w1_hbm, w1), (w2_hbm, w2)))
    ]
    for copy in copies:
        copy.start()
    for f, ref in enumerate((w1, w2)):
        copies[f].wait()
        for m in range(4):
            tiles = [ref[8 * m + u].astype(F32) if 8 * m + u < 27 else jnp.zeros((16, T), F32) for u in range(8)]
            for j, tile in enumerate(regroup(tiles)):
                out[j, 4 * f + m] = tile.astype(BF)


def gathered(ref, k):
    return ref[:, k].reshape(T, T)


def row_of(own, nextx, a, r):
    return (own[a, r] if r < 8 else nextx[a, r - 8]).astype(F32)


def edge_kernel(own, nextx, out):
    first = lanes() < 64
    for a in range(2):
        for p in range(6):
            odd = rolled(row_of(own, nextx, a, 2 * p + 1), 64)
            out[a, p] = jnp.where(first, row_of(own, nextx, a, 2 * p), odd).astype(BF)


def send_kernel(own, nextx, nexty, weights, send):
    for j in range(8):
        for a in range(2):
            for k in range(18):
                send[j, 18 * a + k] = own[a, k] if k < 8 else nextx[a, k - 8] if k < 12 else nexty[a, k - 12]
        for k in range(8):
            send[j, 36 + k] = weights[j, k]


def product(left, right, out, width):
    for n in range(0, width, 640):
        size = min(640, width - n)
        out[:, n : n + size] = jnp.dot(left, right[:, n : n + size], preferred_element_type=F32)


def cells(width):
    lane = lax.broadcasted_iota(jnp.int32, (16, width), 1)
    return lane % 256 // 16, lane % 16


def combine(prods, sign, width, first, place):
    column, depth = cells(width)
    split_y = place[1] == 7
    for step, r in ((1, 8), (-1, 7)):
        a = (1 + sign * step) * 144
        at = 256 * (r - first)
        part = prods[a : a + 144, at : at + 256]
        prods[a : a + 144, at : at + 256] = jnp.where(place[0] == 7, 0.0, part)
    apart = {1: (column == 7) & split_y, -1: (column == 8) & split_y}
    total = None
    for e in range(3):
        part = None
        for c in range(3):
            term = None
            for a in range(3):
                t = 9 * a + 3 * c + e
                start = 256 * a if sign > 0 else 256 * (2 - a)
                piece = prods[t * 16 : t * 16 + 16, start : start + width]
                term = piece if term is None else term + piece
            step = sign * (c - 1)
            if step:
                term = jnp.where(apart[step], 0.0, rolled(term, -step * 16))
            part = term if part is None else part + term
        step = sign * (e - 1)
        if step:
            part = rolled(part, -step)
            part = jnp.where(depth != (15 if step > 0 else 0), part, 0.0)
        total = part if total is None else total + part
    return total


def shifted(field, place, out):
    column, depth = cells(OWN)
    split_y = place[1] == 7
    for c in range(3):
        moved = rolled(field, (c - 1) * 16)
        if c != 1:
            moved = jnp.where((column == (8 if c == 2 else 7)) & split_y, 0.0, moved)
        for e in range(3):
            piece = rolled(moved, e - 1)
            if e != 1:
                piece = jnp.where(depth != (0 if e == 2 else 15), piece, 0.0)
            k = (c * 3 + e) * 16
            out[k : k + 16, :] = piece.astype(BF)


def correlate(place, shifts, field, base, out):
    def product_of(at, start, width):
        return lax.dot_general(
            shifts[:, at : at + width],
            field[:, start : start + width],
            (((1,), (1,)), ((), ())),
            preferred_element_type=F32,
        )

    for a in range(3):
        total = product_of(0, base + 256 * a, OWN)
        if a != 1:
            at = 256 * (5 if a == 2 else 6)
            across = product_of(at, base + 256 * a + at, 256)
            total = total - jnp.where(place[0] == 7, across, 0.0)
        out[a * 144 : a * 144 + 144, :] = total


def gathered_filter(ref, first):
    parts = [gathered(ref, first + m).astype(F32).T.astype(BF) for m in range(4)]
    return jnp.concatenate(parts, axis=0)[0:432]


def first_kernel(place, block, w1rows, send, sums, vol, grad, prods1, prods2, shifts):
    for a, ref in enumerate((vol, grad)):
        def put(tile, value):
            ref[:, tile * T : tile * T + T] = value

        for r in range(12):
            put(2 * r, gathered(block, 18 * a + r))
            value = gathered(block, 18 * a + 12 + r // 2)
            put(2 * r + 1, rolled(value.astype(F32), 64).astype(BF) if r % 2 else value)
    product(w1rows[...].reshape(432, T), vol, prods1, EXT)
    product(gathered_filter(block, 40), grad, prods2, EXT)

    pre = combine(prods1, 1, MID, 0, place).astype(BF).astype(F32)
    sig = jax.nn.sigmoid(pre)
    hidden = (pre * sig).astype(BF).astype(F32)
    back = combine(prods2, -1, MID, 0, place)
    back = (back * sig * (1.0 + pre * (1.0 - sig))).astype(BF).astype(F32)

    narrow = lanes()
    for a, field in enumerate((hidden, back)):
        packed = [None] * 3
        for r in range(10):
            inner = field[:, 2 * r * T : (2 * r + 1) * T]
            outer = field[:, (2 * r + 1) * T : (2 * r + 2) * T]
            tile_r = jnp.where(narrow < 16, rolled(outer, -32), inner).astype(BF)
            q, k = r // 4, r % 4
            moved = rolled(outer, 32 * k)
            packed[q] = moved if packed[q] is None else jnp.where(narrow // 32 == k, moved, packed[q])
            for j in range(8):
                send[j, a * 13 + r] = tile_r
        for q in range(3):
            tile_q = packed[q].astype(BF)
            for j in range(8):
                send[j, a * 13 + 10 + q] = tile_q

    column, _ = cells(OWN)
    inside = (column >= 2) & (column < 10)
    shifted(jnp.where(inside, back[:, 2 * T : 2 * T + OWN], 0.0), place, shifts)
    correlate(place, shifts, vol, 2 * T, sums)


def spread(middle, a, ref):
    lane = lanes(T)
    for r in range(10):
        inner = gathered(middle, a * 13 + r)
        outer = rolled(gathered(middle, a * 13 + 10 + r // 4).astype(F32), -32 * (r % 4))
        ref[:, 2 * r * T : (2 * r + 1) * T] = inner
        outer = jnp.where(lane < 32, outer, rolled(inner.astype(F32), 32))
        ref[:, (2 * r + 1) * T : (2 * r + 2) * T] = outer.astype(BF)


def grad_kernel(place, own, nextx, nexty, middle, sums1, hid, send, field, shifts, sums2):
    spread(middle, 0, hid)
    lane = lanes()
    for r in range(2, 10):
        field[:, (2 * r - 4) * T : (2 * r - 3) * T] = jnp.where(lane >= 32, row_of(own, nextx, 1, r), 0.0)
        tile = nexty[1, r // 2].astype(F32)
        tile = rolled(tile, 64) if r % 2 else tile
        field[:, (2 * r - 3) * T : (2 * r - 2) * T] = jnp.where(lane < 32, tile, 0.0)
    shifted(field[...], place, shifts)
    correlate(place, shifts, hid, 0, sums2)
    rows = jnp.concatenate([sums1[...], sums2[...], jnp.zeros((32, T), F32)], axis=0)
    send[...] = rows.astype(BF).reshape(8, 112, T)


def second_kernel(place, block, middle, hid, w2rows, keep, give, pre, prods):
    spread(middle, 1, pre)

    def store(which, value):
        for x in range(8):
            for side in range(2):
                tile = value[:, (2 * x + side) * T : (2 * x + side + 1) * T].astype(BF)
                if x < 6:
                    keep[which, x, side] = tile
                else:
                    give[which, x - 6, side] = tile

    product(w2rows[...].reshape(432, T), hid, prods, MID)
    store(0, combine(prods, 1, OWN, 1, place))
    product(gathered_filter(block, 36), pre, prods, MID)
    store(1, combine(prods, -1, OWN, 1, place))


def back_kernel(keep, taken, rows, give):
    lane = lanes()
    for a in range(2):
        for q in range(2):
            packed = None
            for k in range(4):
                x = 4 * q + k
                tiles = taken.at[a, x] if x < 2 else keep.at[a, x - 2]
                rows[a, x] = tiles[0]
                moved = rolled(tiles[1].astype(F32), 32 * k)
                packed = moved if packed is None else jnp.where(lane // 32 == k, moved, packed)
            give[a, q] = packed.astype(BF)


def out_kernel(rows, taken, out, vgrad):
    lane = lanes()
    for a, ref in enumerate((out, vgrad)):
        for x in range(8):
            first = rolled(taken[a, x // 4].astype(F32), -32 * (x % 4))
            tile = jnp.where(lane < 32, first, rows[a, x].astype(F32))
            ref[0, x] = tile.T.astype(BF).reshape(8, 16, 16)


def sum_kernel(factor, parts, out):
    total = parts[0].astype(F32)
    for k in range(1, parts.shape[0]):
        total = total + parts[k].astype(F32)
    total = total * factor
    if out.shape == total.shape:
        out[...] = total
    else:
        for j in range(out.shape[0]):
            out[j] = total.astype(BF)


def last_kernel(parts, first, second):
    rows = parts[...].reshape(896, T).astype(F32)
    first[...] = rows[0:432].reshape(27, 16, T)
    second[...] = rows[432:864].reshape(27, 16, T)


def shape(*dims, dtype=BF):
    return jax.ShapeDtypeStruct(dims, dtype)


def cyclic(x, axis, step):
    size = lax.axis_size(axis)
    return lax.ppermute(x, axis, [(i, (i + step) % size) for i in range(size)])


def on_device(volume, first_filter, second_filter, out_grad):
    factor = 1.0 / math.sqrt(64 * 64 * 16)
    place = jnp.stack([lax.axis_index("gx"), lax.axis_index(GY)]).astype(jnp.int32)
    w1 = first_filter.transpose(1, 0, 2)
    w2 = second_filter.transpose(1, 0, 2)
    two = shape(2, 8, 16, T)
    own, low = call(
        pack_kernel,
        (two, shape(2, 4, 16, T)),
        [pltpu.VMEM((1, 8, 8, 16, 16), BF)] * 2 + [pltpu.SemaphoreType.DMA((2,))],
        hbm=True,
    )(volume, out_grad)
    nextx = cyclic(low, "gx", -1)
    pieces = call(
        weight_kernel,
        shape(8, 8, 16, T),
        [pltpu.VMEM((27, 16, T), BF)] * 2 + [pltpu.SemaphoreType.DMA((2,))],
        hbm=True,
    )(w1, w2)
    nextx, pieces = lax.optimization_barrier((nextx, pieces))
    nexty = cyclic(call(edge_kernel, shape(2, 6, 16, T))(own, nextx), GY, -1)
    nexty, place = lax.optimization_barrier((nexty, place))
    block = lax.all_to_all(call(send_kernel, shape(8, 44, 16, T))(own, nextx, nexty, pieces), "af", 0, 0)
    middle, sums = call(
        first_kernel,
        (shape(8, 26, 16, T), shape(432, T, dtype=F32)),
        [
            pltpu.VMEM((T, EXT), BF),
            pltpu.VMEM((T, EXT), BF),
            pltpu.VMEM((432, EXT), F32),
            pltpu.VMEM((432, EXT), F32),
            pltpu.VMEM((144, OWN), BF),
        ],
        scalars=True,
        limit=28,
    )(place, block, w1)
    middle = lax.all_to_all(middle, "af", 0, 0)
    many = shape(8, 112, T)
    hid, parts = call(
        grad_kernel,
        (shape(T, MID), many),
        [pltpu.VMEM((16, OWN), F32), pltpu.VMEM((144, OWN), BF), pltpu.VMEM((432, T), F32)],
        scalars=True,
        limit=16,
    )(place, own, nextx, nexty, middle, sums)
    keep, give = call(
        second_kernel,
        (shape(2, 6, 2, 16, T), shape(2, 2, 2, 16, T)),
        [pltpu.VMEM((T, MID), BF), pltpu.VMEM((432, MID), F32)],
        scalars=True,
        limit=20,
    )(place, block, middle, hid, w2)
    parts = lax.all_to_all(parts, "gx", 0, 0)
    parts, keep, give = lax.optimization_barrier((parts, keep, give))
    parts = call(functools.partial(sum_kernel, 1.0), many)(parts)
    rows, give = call(back_kernel, (two, shape(2, 2, 16, T)))(keep, cyclic(give, "gx", 1))
    parts = lax.all_to_all(parts, GY, 0, 0)
    parts, rows, give = lax.optimization_barrier((parts, rows, give))
    parts = call(functools.partial(sum_kernel, factor), many)(parts)
    output, volume_grad = call(out_kernel, (shape(1, 8, 8, 16, 16), shape(1, 8, 8, 16, 16)))(rows, cyclic(give, GY, 1))
    parts = lax.all_to_all(parts, "gx", 0, 0)
    wide = shape(27, 16, T, dtype=F32)
    first_grad, second_grad = call(last_kernel, (wide, wide))(parts)
    return output, volume_grad, first_grad.transpose(1, 0, 2), second_grad.transpose(1, 0, 2)


def solution(mesh):
    split = jax.sharding.Mesh(mesh.devices.reshape(8, 4, 2, 8), ("gx", "yh", "co", "af"))
    cells = P(None, "gx", GY, None, "af")
    weights = P("af", None, None)
    return jax.shard_map(
        on_device,
        mesh=split,
        in_specs=(cells, weights, weights, cells),
        out_specs=(cells, cells, weights, weights),
        check_vma=False,
    )
```

```python
import functools
import math

import jax
import jax.numpy as jnp
from jax import lax
from jax.experimental import pallas as pl
from jax.experimental.pallas import tpu as pltpu
from jax.sharding import PartitionSpec as P

BF = jnp.bfloat16
F32 = jnp.float32
T = 128
VMEM = pl.BlockSpec(memory_space=pltpu.VMEM)
SMEM = pl.BlockSpec(memory_space=pltpu.SMEM)
HBM = pl.BlockSpec(memory_space=pltpu.HBM)
GY = ("yh", "co")
MID = 20 * T
OWN = 16 * T


def call(kernel, outs, scratch=(), scalars=False, hbm=False, limit=8):
    def run(*args):
        return pl.pallas_call(
            kernel,
            out_shape=outs,
            in_specs=[HBM if hbm else SMEM if scalars and k == 0 else VMEM for k in range(len(args))],
            scratch_shapes=scratch,
            compiler_params=pltpu.CompilerParams(vmem_limit_bytes=limit << 20),
        )(*args)

    return run


def lanes(rows=16):
    return lax.broadcasted_iota(jnp.int32, (rows, T), 1)


def rolled(x, shift):
    size = x.shape[1]
    return pltpu.roll(x, shift % size, 1) if shift % size else x


def regroup(tiles):
    lane = lanes()
    tiles = list(tiles)
    for bit in (1, 2, 4):
        clear = (lane // (16 * bit)) % 2 == 0
        for u in range(8):
            if u & bit:
                continue
            first, second = tiles[u], tiles[u + bit]
            tiles[u] = jnp.where(clear, first, rolled(second, 16 * bit))
            tiles[u + bit] = jnp.where(clear, rolled(first, -16 * bit), second)
    return tiles


def pack_kernel(vol_hbm, grad_hbm, own, low, vol, grad, sems):
    copies = [
        pltpu.make_async_copy(source, target, sems.at[k])
        for k, (source, target) in enumerate(((vol_hbm, vol), (grad_hbm, grad)))
    ]
    for copy in copies:
        copy.start()
    for a, ref in enumerate((vol, grad)):
        copies[a].wait()
        for x in range(8):
            tile = ref[0, x].reshape(T, 16).astype(F32).T.astype(BF)
            own[a, x] = tile
            if x < 4:
                low[a, x] = tile


def weight_kernel(w1_hbm, w2_hbm, out, w1, w2, sems):
    copies = [
        pltpu.make_async_copy(source, target, sems.at[k])
        for k, (source, target) in enumerate(((w1_hbm, w1), (w2_hbm, w2)))
    ]
    for copy in copies:
        copy.start()
    for f, ref in enumerate((w1, w2)):
        copies[f].wait()
        for m in range(4):
            tiles = [ref[8 * m + u].astype(F32) if 8 * m + u < 27 else jnp.zeros((16, T), F32) for u in range(8)]
            for j, tile in enumerate(regroup(tiles)):
                out[j, 4 * f + m] = tile.astype(BF)


def gathered(ref, k):
    return ref[:, k].reshape(T, T)


def row_of(own, nextx, a, r):
    return (own[a, r] if r < 8 else nextx[a, r - 8]).astype(F32)


def edge_kernel(own, nextx, out):
    first = lanes() < 64
    for a in range(2):
        for p in range(6):
            odd = rolled(row_of(own, nextx, a, 2 * p + 1), 64)
            out[a, p] = jnp.where(first, row_of(own, nextx, a, 2 * p), odd).astype(BF)


def send_kernel(own, nextx, nexty, weights, send):
    for j in range(8):
        for a in range(2):
            for k in range(18):
                send[j, 18 * a + k] = own[a, k] if k < 8 else nextx[a, k - 8] if k < 12 else nexty[a, k - 12]
        for k in range(8):
            send[j, 36 + k] = weights[j, k]


def product(left, right, out, width):
    for n in range(0, width, 640):
        size = min(640, width - n)
        out[:, n : n + size] = jnp.dot(left, right[:, n : n + size], preferred_element_type=F32)


def cells(width):
    lane = lax.broadcasted_iota(jnp.int32, (16, width), 1)
    return lane % 256 // 16, lane % 16


def stacked(place, ref, first, count, r, side, value):
    for b in range(3):
        out_row = r - b + 1
        if not first <= out_row < first + count:
            continue
        if (b, out_row) in ((2, 7), (0, 8)):
            tile = (value.astype(F32) * jnp.where(place[0] == 7, 0.0, 1.0)).astype(BF)
        else:
            tile = value
        at = (2 * (out_row - first) + side) * T
        ref[b * T : b * T + T, at : at + T] = tile


def combine(prods, sign, width, place):
    column, depth = cells(width)
    split_y = place[1] == 7
    apart = {1: (column == 7) & split_y, -1: (column == 8) & split_y}
    total = None
    for e in range(3):
        part = None
        for c in range(3):
            k = (3 * c + e) * 16
            term = prods[k : k + 16, :]
            step = sign * (c - 1)
            if step:
                term = jnp.where(apart[step], 0.0, rolled(term, -step * 16))
            part = term if part is None else part + term
        step = sign * (e - 1)
        if step:
            part = rolled(part, -step)
            part = jnp.where(depth != (15 if step > 0 else 0), part, 0.0)
        total = part if total is None else total + part
    return total


def shifted(field, place, out):
    column, depth = cells(OWN)
    split_y = place[1] == 7
    for c in range(3):
        moved = rolled(field, (c - 1) * 16)
        if c != 1:
            moved = jnp.where((column == (8 if c == 2 else 7)) & split_y, 0.0, moved)
        for e in range(3):
            piece = rolled(moved, e - 1)
            if e != 1:
                piece = jnp.where(depth != (0 if e == 2 else 15), piece, 0.0)
            k = (c * 3 + e) * 16
            out[k : k + 16, :] = piece.astype(BF)


def correlate(shifts, field, out):
    total = lax.dot_general(shifts[...], field, (((1,), (1,)), ((), ())), preferred_element_type=F32)
    for a in range(3):
        out[a * 144 : a * 144 + 144, :] = total[:, a * T : a * T + T]


def by_tap(filters, sign):
    parts = [filters[a * 144 : a * 144 + 144] for a in range(3)]
    return jnp.concatenate(parts[::sign], axis=1)


def gathered_filter(ref, first):
    parts = [gathered(ref, first + m).astype(F32).T.astype(BF) for m in range(4)]
    return jnp.concatenate(parts, axis=0)[0:432]


def first_kernel(place, block, w1rows, send, sums, vol, grad, prods1, prods2, shifts):
    for a, ref in enumerate((vol, grad)):
        for r in range(12):
            value = gathered(block, 18 * a + 12 + r // 2)
            value = rolled(value.astype(F32), 64).astype(BF) if r % 2 else value
            stacked(place, ref, 1, 10, r, 0, gathered(block, 18 * a + r))
            stacked(place, ref, 1, 10, r, 1, value)
    product(by_tap(w1rows[...].reshape(432, T), 1), vol, prods1, MID)
    product(by_tap(gathered_filter(block, 40), -1), grad, prods2, MID)

    pre = combine(prods1, 1, MID, place).astype(BF).astype(F32)
    sig = jax.nn.sigmoid(pre)
    hidden = (pre * sig).astype(BF).astype(F32)
    back = combine(prods2, -1, MID, place)
    back = (back * sig * (1.0 + pre * (1.0 - sig))).astype(BF).astype(F32)

    narrow = lanes()
    for a, field in enumerate((hidden, back)):
        packed = [None] * 3
        for r in range(10):
            inner = field[:, 2 * r * T : (2 * r + 1) * T]
            outer = field[:, (2 * r + 1) * T : (2 * r + 2) * T]
            tile_r = jnp.where(narrow < 16, rolled(outer, -32), inner).astype(BF)
            q, k = r // 4, r % 4
            moved = rolled(outer, 32 * k)
            packed[q] = moved if packed[q] is None else jnp.where(narrow // 32 == k, moved, packed[q])
            for j in range(8):
                send[j, a * 13 + r] = tile_r
        for q in range(3):
            tile_q = packed[q].astype(BF)
            for j in range(8):
                send[j, a * 13 + 10 + q] = tile_q

    column, _ = cells(OWN)
    inside = (column >= 2) & (column < 10)
    shifted(jnp.where(inside, back[:, 2 * T : 2 * T + OWN], 0.0), place, shifts)
    correlate(shifts, vol[:, 2 * T : 2 * T + OWN], sums)


def spread(place, middle, a, ref):
    lane = lanes(T)
    for r in range(10):
        inner = gathered(middle, a * 13 + r)
        outer = rolled(gathered(middle, a * 13 + 10 + r // 4).astype(F32), -32 * (r % 4))
        outer = jnp.where(lane < 32, outer, rolled(inner.astype(F32), 32)).astype(BF)
        stacked(place, ref, 2, 8, r + 1, 0, inner)
        stacked(place, ref, 2, 8, r + 1, 1, outer)


def grad_kernel(place, own, nextx, nexty, middle, sums1, send, hid, field, shifts, sums2):
    spread(place, middle, 0, hid)
    lane = lanes()
    for r in range(2, 10):
        field[:, (2 * r - 4) * T : (2 * r - 3) * T] = jnp.where(lane >= 32, row_of(own, nextx, 1, r), 0.0)
        tile = nexty[1, r // 2].astype(F32)
        tile = rolled(tile, 64) if r % 2 else tile
        field[:, (2 * r - 3) * T : (2 * r - 2) * T] = jnp.where(lane < 32, tile, 0.0)
    shifted(field[...], place, shifts)
    correlate(shifts, hid[...], sums2)
    rows = jnp.concatenate([sums1[...], sums2[...], jnp.zeros((32, T), F32)], axis=0)
    send[...] = rows.astype(BF).reshape(8, 112, T)


def second_kernel(place, block, middle, w2rows, keep, give, hid, pre, prods):
    spread(place, middle, 0, hid)
    spread(place, middle, 1, pre)

    def store(which, value):
        for x in range(8):
            for side in range(2):
                tile = value[:, (2 * x + side) * T : (2 * x + side + 1) * T].astype(BF)
                if x < 6:
                    keep[which, x, side] = tile
                else:
                    give[which, x - 6, side] = tile

    product(by_tap(w2rows[...].reshape(432, T), 1), hid, prods, OWN)
    store(0, combine(prods, 1, OWN, place))
    product(by_tap(gathered_filter(block, 36), -1), pre, prods, OWN)
    store(1, combine(prods, -1, OWN, place))


def back_kernel(keep, taken, rows, give):
    lane = lanes()
    for a in range(2):
        for q in range(2):
            packed = None
            for k in range(4):
                x = 4 * q + k
                tiles = taken.at[a, x] if x < 2 else keep.at[a, x - 2]
                rows[a, x] = tiles[0]
                moved = rolled(tiles[1].astype(F32), 32 * k)
                packed = moved if packed is None else jnp.where(lane // 32 == k, moved, packed)
            give[a, q] = packed.astype(BF)


def out_kernel(rows, taken, out, vgrad):
    lane = lanes()
    for a, ref in enumerate((out, vgrad)):
        for x in range(8):
            first = rolled(taken[a, x // 4].astype(F32), -32 * (x % 4))
            tile = jnp.where(lane < 32, first, rows[a, x].astype(F32))
            ref[0, x] = tile.T.astype(BF).reshape(8, 16, 16)


def sum_kernel(factor, parts, out):
    total = parts[0].astype(F32)
    for k in range(1, parts.shape[0]):
        total = total + parts[k].astype(F32)
    total = total * factor
    if out.shape == total.shape:
        out[...] = total
    else:
        for j in range(out.shape[0]):
            out[j] = total.astype(BF)


def last_kernel(parts, first, second):
    rows = parts[...].reshape(896, T).astype(F32)
    first[...] = rows[0:432].reshape(27, 16, T)
    second[...] = rows[432:864].reshape(27, 16, T)


def shape(*dims, dtype=BF):
    return jax.ShapeDtypeStruct(dims, dtype)


def cyclic(x, axis, step):
    size = lax.axis_size(axis)
    return lax.ppermute(x, axis, [(i, (i + step) % size) for i in range(size)])


def on_device(volume, first_filter, second_filter, out_grad):
    factor = 1.0 / math.sqrt(64 * 64 * 16)
    place = jnp.stack([lax.axis_index("gx"), lax.axis_index(GY)]).astype(jnp.int32)
    w1 = first_filter.transpose(1, 0, 2)
    w2 = second_filter.transpose(1, 0, 2)
    two = shape(2, 8, 16, T)
    own, low = call(
        pack_kernel,
        (two, shape(2, 4, 16, T)),
        [pltpu.VMEM((1, 8, 8, 16, 16), BF)] * 2 + [pltpu.SemaphoreType.DMA((2,))],
        hbm=True,
    )(volume, out_grad)
    nextx = cyclic(low, "gx", -1)
    pieces = call(
        weight_kernel,
        shape(8, 8, 16, T),
        [pltpu.VMEM((27, 16, T), BF)] * 2 + [pltpu.SemaphoreType.DMA((2,))],
        hbm=True,
    )(w1, w2)
    nextx, pieces = lax.optimization_barrier((nextx, pieces))
    nexty = cyclic(call(edge_kernel, shape(2, 6, 16, T))(own, nextx), GY, -1)
    nexty, place = lax.optimization_barrier((nexty, place))
    block = lax.all_to_all(call(send_kernel, shape(8, 44, 16, T))(own, nextx, nexty, pieces), "af", 0, 0)
    middle, sums = call(
        first_kernel,
        (shape(8, 26, 16, T), shape(432, T, dtype=F32)),
        [
            pltpu.VMEM((3 * T, MID), BF),
            pltpu.VMEM((3 * T, MID), BF),
            pltpu.VMEM((144, MID), F32),
            pltpu.VMEM((144, MID), F32),
            pltpu.VMEM((144, OWN), BF),
        ],
        scalars=True,
        limit=28,
    )(place, block, w1)
    middle = lax.all_to_all(middle, "af", 0, 0)
    many = shape(8, 112, T)
    parts = call(
        grad_kernel,
        many,
        [
            pltpu.VMEM((3 * T, OWN), BF),
            pltpu.VMEM((16, OWN), F32),
            pltpu.VMEM((144, OWN), BF),
            pltpu.VMEM((432, T), F32),
        ],
        scalars=True,
        limit=16,
    )(place, own, nextx, nexty, middle, sums)
    keep, give = call(
        second_kernel,
        (shape(2, 6, 2, 16, T), shape(2, 2, 2, 16, T)),
        [pltpu.VMEM((3 * T, OWN), BF)] * 2 + [pltpu.VMEM((144, OWN), F32)],
        scalars=True,
        limit=20,
    )(place, block, middle, w2)
    parts = lax.all_to_all(parts, "gx", 0, 0)
    parts, keep, give = lax.optimization_barrier((parts, keep, give))
    parts = call(functools.partial(sum_kernel, 1.0), many)(parts)
    rows, give = call(back_kernel, (two, shape(2, 2, 16, T)))(keep, cyclic(give, "gx", 1))
    parts = lax.all_to_all(parts, GY, 0, 0)
    parts, rows, give = lax.optimization_barrier((parts, rows, give))
    parts = call(functools.partial(sum_kernel, factor), many)(parts)
    output, volume_grad = call(out_kernel, (shape(1, 8, 8, 16, 16), shape(1, 8, 8, 16, 16)))(rows, cyclic(give, GY, 1))
    parts = lax.all_to_all(parts, "gx", 0, 0)
    wide = shape(27, 16, T, dtype=F32)
    first_grad, second_grad = call(last_kernel, (wide, wide))(parts)
    return output, volume_grad, first_grad.transpose(1, 0, 2), second_grad.transpose(1, 0, 2)


def solution(mesh):
    split = jax.sharding.Mesh(mesh.devices.reshape(8, 4, 2, 8), ("gx", "yh", "co", "af"))
    cells = P(None, "gx", GY, None, "af")
    weights = P("af", None, None)
    return jax.shard_map(
        on_device,
        mesh=split,
        in_specs=(cells, weights, weights, cells),
        out_specs=(cells, cells, weights, weights),
        check_vma=False,
    )
```

```python
import functools
import math

import jax
import jax.numpy as jnp
from jax import lax
from jax.experimental import pallas as pl
from jax.experimental.pallas import tpu as pltpu
from jax.sharding import PartitionSpec as P

BF = jnp.bfloat16
F32 = jnp.float32
T = 128
VMEM = pl.BlockSpec(memory_space=pltpu.VMEM)
SMEM = pl.BlockSpec(memory_space=pltpu.SMEM)
HBM = pl.BlockSpec(memory_space=pltpu.HBM)
GY = ("yh", "co")
MID = 20 * T
OWN = 16 * T


def call(kernel, outs, scratch=(), scalars=False, hbm=False, limit=8):
    def run(*args):
        return pl.pallas_call(
            kernel,
            out_shape=outs,
            in_specs=[HBM if hbm else SMEM if scalars and k == 0 else VMEM for k in range(len(args))],
            scratch_shapes=scratch,
            compiler_params=pltpu.CompilerParams(vmem_limit_bytes=limit << 20),
        )(*args)

    return run


def lanes(rows=16):
    return lax.broadcasted_iota(jnp.int32, (rows, T), 1)


def rolled(x, shift):
    size = x.shape[1]
    return pltpu.roll(x, shift % size, 1) if shift % size else x


def regroup(tiles):
    lane = lanes()
    tiles = list(tiles)
    for bit in (1, 2, 4):
        clear = (lane // (16 * bit)) % 2 == 0
        for u in range(8):
            if u & bit:
                continue
            first, second = tiles[u], tiles[u + bit]
            tiles[u] = jnp.where(clear, first, rolled(second, 16 * bit))
            tiles[u + bit] = jnp.where(clear, rolled(first, -16 * bit), second)
    return tiles


def pack_kernel(vol_hbm, grad_hbm, own, low, vol, grad, sems):
    copies = [
        pltpu.make_async_copy(source, target, sems.at[k])
        for k, (source, target) in enumerate(((vol_hbm, vol), (grad_hbm, grad)))
    ]
    for copy in copies:
        copy.start()
    for a, ref in enumerate((vol, grad)):
        copies[a].wait()
        for x in range(8):
            tile = ref[0, x].reshape(T, 16).astype(F32).T.astype(BF)
            own[a, x] = tile
            if x < 4:
                low[a, x] = tile


def weight_kernel(w1_hbm, w2_hbm, out, w1, w2, sems):
    copies = [
        pltpu.make_async_copy(source, target, sems.at[k])
        for k, (source, target) in enumerate(((w1_hbm, w1), (w2_hbm, w2)))
    ]
    for copy in copies:
        copy.start()
    for f, ref in enumerate((w1, w2)):
        copies[f].wait()
        for m in range(4):
            tiles = [ref[8 * m + u].astype(F32) if 8 * m + u < 27 else jnp.zeros((16, T), F32) for u in range(8)]
            for j, tile in enumerate(regroup(tiles)):
                out[j, 4 * f + m] = tile.astype(BF)


def gathered(ref, k):
    return ref[:, k].reshape(T, T)


def row_of(own, nextx, a, r):
    return (own[a, r] if r < 8 else nextx[a, r - 8]).astype(F32)


def edge_kernel(own, nextx, out):
    first = lanes() < 64
    for a in range(2):
        for p in range(6):
            odd = rolled(row_of(own, nextx, a, 2 * p + 1), 64)
            out[a, p] = jnp.where(first, row_of(own, nextx, a, 2 * p), odd).astype(BF)


def send_kernel(own, nextx, nexty, weights, send):
    for j in range(8):
        for a in range(2):
            for k in range(18):
                send[j, 18 * a + k] = own[a, k] if k < 8 else nextx[a, k - 8] if k < 12 else nexty[a, k - 12]
        for k in range(8):
            send[j, 36 + k] = weights[j, k]


def product(left, right, out, width):
    for n in range(0, width, 640):
        size = min(640, width - n)
        out[:, n : n + size] = jnp.dot(left, right[:, n : n + size], preferred_element_type=F32)


def cells(width):
    lane = lax.broadcasted_iota(jnp.int32, (16, width), 1)
    return lane % 256 // 16, lane % 16


def stacked(place, ref, first, count, r, side, value):
    for b in range(3):
        out_row = r - b + 1
        if not first <= out_row < first + count:
            continue
        if (b, out_row) in ((2, 7), (0, 8)):
            tile = (value.astype(F32) * jnp.where(place[0] == 7, 0.0, 1.0)).astype(BF)
        else:
            tile = value
        at = (2 * (out_row - first) + side) * T
        ref[b * T : b * T + T, at : at + T] = tile


def combine(prods, sign, width, place):
    column, depth = cells(width)
    split_y = place[1] == 7
    apart = {1: (column == 7) & split_y, -1: (column == 8) & split_y}
    total = None
    for e in range(3):
        part = None
        for c in range(3):
            k = (3 * c + e) * 16
            term = prods[k : k + 16, :]
            step = sign * (c - 1)
            if step:
                term = jnp.where(apart[step], 0.0, rolled(term, -step * 16))
            part = term if part is None else part + term
        step = sign * (e - 1)
        if step:
            part = rolled(part, -step)
            part = jnp.where(depth != (15 if step > 0 else 0), part, 0.0)
        total = part if total is None else total + part
    return total


def shifted(field, place, out):
    column, depth = cells(OWN)
    split_y = place[1] == 7
    for c in range(3):
        moved = rolled(field, (c - 1) * 16)
        if c != 1:
            moved = jnp.where((column == (8 if c == 2 else 7)) & split_y, 0.0, moved)
        for e in range(3):
            piece = rolled(moved, e - 1)
            if e != 1:
                piece = jnp.where(depth != (0 if e == 2 else 15), piece, 0.0)
            k = (c * 3 + e) * 16
            out[k : k + 16, :] = piece.astype(BF)


def correlate(shifts, field, out):
    total = lax.dot_general(shifts[...], field, (((1,), (1,)), ((), ())), preferred_element_type=F32)
    for a in range(3):
        out[a * 144 : a * 144 + 144, :] = total[:, a * T : a * T + T]


def by_tap(filters, sign):
    parts = [filters[a * 144 : a * 144 + 144] for a in range(3)]
    return jnp.concatenate(parts[::sign], axis=1)


def gathered_filter(ref, first):
    parts = [gathered(ref, first + m).astype(F32).T.astype(BF) for m in range(4)]
    return jnp.concatenate(parts, axis=0)[0:432]


def first_kernel(place, block, w1rows, send, sums, vol, grad, prods1, prods2, shifts):
    for a, ref in enumerate((vol, grad)):
        for r in range(12):
            value = gathered(block, 18 * a + 12 + r // 2)
            value = rolled(value.astype(F32), 64).astype(BF) if r % 2 else value
            stacked(place, ref, 1, 10, r, 0, gathered(block, 18 * a + r))
            stacked(place, ref, 1, 10, r, 1, value)
    product(by_tap(w1rows[...].reshape(432, T), 1), vol, prods1, MID)
    product(by_tap(gathered_filter(block, 40), -1), grad, prods2, MID)

    pre = combine(prods1, 1, MID, place).astype(BF).astype(F32)
    sig = jax.nn.sigmoid(pre)
    hidden = (pre * sig).astype(BF).astype(F32)
    back = combine(prods2, -1, MID, place)
    back = (back * sig * (1.0 + pre * (1.0 - sig))).astype(BF).astype(F32)

    narrow = lanes()
    for a, field in enumerate((hidden, back)):
        packed = [None] * 3
        for r in range(10):
            inner = field[:, 2 * r * T : (2 * r + 1) * T]
            outer = field[:, (2 * r + 1) * T : (2 * r + 2) * T]
            tile_r = jnp.where(narrow < 16, rolled(outer, -32), inner).astype(BF)
            q, k = r // 4, r % 4
            moved = rolled(outer, 32 * k)
            packed[q] = moved if packed[q] is None else jnp.where(narrow // 32 == k, moved, packed[q])
            for j in range(8):
                send[j, a * 13 + r] = tile_r
        for q in range(3):
            tile_q = packed[q].astype(BF)
            for j in range(8):
                send[j, a * 13 + 10 + q] = tile_q

    column, _ = cells(OWN)
    inside = (column >= 2) & (column < 10)
    shifted(jnp.where(inside, back[:, 2 * T : 2 * T + OWN], 0.0), place, shifts)
    correlate(shifts, vol[:, 2 * T : 2 * T + OWN], sums)


def spread(place, middle, a, ref):
    lane = lanes(T)
    for r in range(10):
        inner = gathered(middle, a * 13 + r)
        outer = rolled(gathered(middle, a * 13 + 10 + r // 4).astype(F32), -32 * (r % 4))
        outer = jnp.where(lane < 32, outer, rolled(inner.astype(F32), 32)).astype(BF)
        stacked(place, ref, 2, 8, r + 1, 0, inner)
        stacked(place, ref, 2, 8, r + 1, 1, outer)


def grad_kernel(place, own, nextx, nexty, middle, sums1, send, hid, field, shifts, sums2):
    spread(place, middle, 0, hid)
    lane = lanes()
    for r in range(2, 10):
        field[:, (2 * r - 4) * T : (2 * r - 3) * T] = jnp.where(lane >= 32, row_of(own, nextx, 1, r), 0.0)
        tile = nexty[1, r // 2].astype(F32)
        tile = rolled(tile, 64) if r % 2 else tile
        field[:, (2 * r - 3) * T : (2 * r - 2) * T] = jnp.where(lane < 32, tile, 0.0)
    shifted(field[...], place, shifts)
    correlate(shifts, hid[...], sums2)
    rows = jnp.concatenate([sums1[...], sums2[...], jnp.zeros((32, T), F32)], axis=0)
    send[...] = rows.astype(BF).reshape(8, 112, T)


def second_kernel(place, block, middle, w2rows, keep, give, hid, pre, prods):
    spread(place, middle, 0, hid)
    spread(place, middle, 1, pre)

    def store(which, value):
        for x in range(8):
            for side in range(2):
                tile = value[:, (2 * x + side) * T : (2 * x + side + 1) * T].astype(BF)
                if x < 6:
                    keep[which, x, side] = tile
                else:
                    give[which, x - 6, side] = tile

    product(by_tap(w2rows[...].reshape(432, T), 1), hid, prods, OWN)
    store(0, combine(prods, 1, OWN, place))
    product(by_tap(gathered_filter(block, 36), -1), pre, prods, OWN)
    store(1, combine(prods, -1, OWN, place))


def back_kernel(keep, taken, rows, give):
    lane = lanes()
    for a in range(2):
        for q in range(2):
            packed = None
            for k in range(4):
                x = 4 * q + k
                tiles = taken.at[a, x] if x < 2 else keep.at[a, x - 2]
                rows[a, x] = tiles[0]
                moved = rolled(tiles[1].astype(F32), 32 * k)
                packed = moved if packed is None else jnp.where(lane // 32 == k, moved, packed)
            give[a, q] = packed.astype(BF)


def out_kernel(rows, taken, out, vgrad):
    lane = lanes()
    for a, ref in enumerate((out, vgrad)):
        for x in range(8):
            first = rolled(taken[a, x // 4].astype(F32), -32 * (x % 4))
            tile = jnp.where(lane < 32, first, rows[a, x].astype(F32))
            ref[0, x] = tile.T.astype(BF).reshape(8, 16, 16)


def sum_kernel(factor, parts, out):
    total = parts[0].astype(F32)
    for k in range(1, parts.shape[0]):
        total = total + parts[k].astype(F32)
    total = total * factor
    if out.shape == total.shape:
        out[...] = total
    else:
        for j in range(out.shape[0]):
            out[j] = total.astype(BF)


def last_kernel(parts, first, second):
    rows = parts[...].reshape(896, T).astype(F32)
    first[...] = rows[0:432].reshape(27, 16, T)
    second[...] = rows[432:864].reshape(27, 16, T)


def shape(*dims, dtype=BF):
    return jax.ShapeDtypeStruct(dims, dtype)


def cyclic(x, axis, step):
    size = lax.axis_size(axis)
    return lax.ppermute(x, axis, [(i, (i + step) % size) for i in range(size)])


def on_device(volume, first_filter, second_filter, out_grad):
    factor = 1.0 / math.sqrt(64 * 64 * 16)
    place = jnp.stack([lax.axis_index("gx"), lax.axis_index(GY)]).astype(jnp.int32)
    w1 = first_filter.transpose(1, 0, 2)
    w2 = second_filter.transpose(1, 0, 2)
    two = shape(2, 8, 16, T)
    own, low = call(
        pack_kernel,
        (two, shape(2, 4, 16, T)),
        [pltpu.VMEM((1, 8, 8, 16, 16), BF)] * 2 + [pltpu.SemaphoreType.DMA((2,))],
        hbm=True,
    )(volume, out_grad)
    nextx = cyclic(low, "gx", -1)
    pieces = call(
        weight_kernel,
        shape(8, 8, 16, T),
        [pltpu.VMEM((27, 16, T), BF)] * 2 + [pltpu.SemaphoreType.DMA((2,))],
        hbm=True,
    )(w1, w2)
    nextx, pieces = lax.optimization_barrier((nextx, pieces))
    nexty = cyclic(call(edge_kernel, shape(2, 6, 16, T))(own, nextx), GY, -1)
    nexty, place = lax.optimization_barrier((nexty, place))
    block = lax.all_to_all(call(send_kernel, shape(8, 44, 16, T))(own, nextx, nexty, pieces), "af", 0, 0)
    middle, sums = call(
        first_kernel,
        (shape(8, 26, 16, T), shape(432, T, dtype=F32)),
        [
            pltpu.VMEM((3 * T, MID), BF),
            pltpu.VMEM((3 * T, MID), BF),
            pltpu.VMEM((144, MID), F32),
            pltpu.VMEM((144, MID), F32),
            pltpu.VMEM((144, OWN), BF),
        ],
        scalars=True,
        limit=28,
    )(place, block, w1)
    middle = lax.all_to_all(middle, "af", 0, 0)
    many = shape(8, 112, T)
    parts = call(
        grad_kernel,
        many,
        [
            pltpu.VMEM((3 * T, OWN), BF),
            pltpu.VMEM((16, OWN), F32),
            pltpu.VMEM((144, OWN), BF),
            pltpu.VMEM((432, T), F32),
        ],
        scalars=True,
        limit=16,
    )(place, own, nextx, nexty, middle, sums)
    keep, give = call(
        second_kernel,
        (shape(2, 6, 2, 16, T), shape(2, 2, 2, 16, T)),
        [pltpu.VMEM((3 * T, OWN), BF)] * 2 + [pltpu.VMEM((144, OWN), F32)],
        scalars=True,
        limit=20,
    )(place, block, middle, w2)
    parts = lax.all_to_all(parts, "gx", 0, 0, axis_index_groups=[[0, 4, 1, 5, 2, 6, 3, 7]])
    parts, keep, give = lax.optimization_barrier((parts, keep, give))
    parts = call(functools.partial(sum_kernel, 1.0), many)(parts)
    rows, give = call(back_kernel, (two, shape(2, 2, 16, T)))(keep, cyclic(give, "gx", 1))
    parts = lax.all_to_all(parts, GY, 0, 0)
    parts, rows, give = lax.optimization_barrier((parts, rows, give))
    parts = call(functools.partial(sum_kernel, factor), many)(parts)
    output, volume_grad = call(out_kernel, (shape(1, 8, 8, 16, 16), shape(1, 8, 8, 16, 16)))(rows, cyclic(give, GY, 1))
    parts = lax.all_to_all(parts, "gx", 0, 0, axis_index_groups=[[0, 4, 1, 5, 2, 6, 3, 7]])
    wide = shape(27, 16, T, dtype=F32)
    first_grad, second_grad = call(last_kernel, (wide, wide))(parts)
    return output, volume_grad, first_grad.transpose(1, 0, 2), second_grad.transpose(1, 0, 2)


def solution(mesh):
    split = jax.sharding.Mesh(mesh.devices.reshape(8, 4, 2, 8), ("gx", "yh", "co", "af"))
    cells = P(None, "gx", GY, None, "af")
    weights = P("af", None, None)
    return jax.shard_map(
        on_device,
        mesh=split,
        in_specs=(cells, weights, weights, cells),
        out_specs=(cells, cells, weights, weights),
        check_vma=False,
    )
```

```python
import functools
import math

import jax
import jax.numpy as jnp
from jax import lax
from jax.experimental import pallas as pl
from jax.experimental.pallas import tpu as pltpu
from jax.sharding import PartitionSpec as P

BF = jnp.bfloat16
F32 = jnp.float32
T = 128
VMEM = pl.BlockSpec(memory_space=pltpu.VMEM)
SMEM = pl.BlockSpec(memory_space=pltpu.SMEM)
HBM = pl.BlockSpec(memory_space=pltpu.HBM)
GY = ("y1", "y0", "co")
MID = 20 * T
OWN = 16 * T


def call(kernel, outs, scratch=(), scalars=False, hbm=False, limit=8):
    def run(*args):
        return pl.pallas_call(
            kernel,
            out_shape=outs,
            in_specs=[HBM if hbm else SMEM if scalars and k == 0 else VMEM for k in range(len(args))],
            scratch_shapes=scratch,
            compiler_params=pltpu.CompilerParams(vmem_limit_bytes=limit << 20),
        )(*args)

    return run


def lanes(rows=16):
    return lax.broadcasted_iota(jnp.int32, (rows, T), 1)


def rolled(x, shift):
    size = x.shape[1]
    return pltpu.roll(x, shift % size, 1) if shift % size else x


def regroup(tiles):
    lane = lanes()
    tiles = list(tiles)
    for bit in (1, 2, 4):
        clear = (lane // (16 * bit)) % 2 == 0
        for u in range(8):
            if u & bit:
                continue
            first, second = tiles[u], tiles[u + bit]
            tiles[u] = jnp.where(clear, first, rolled(second, 16 * bit))
            tiles[u + bit] = jnp.where(clear, rolled(first, -16 * bit), second)
    return tiles


def pack_kernel(vol_hbm, grad_hbm, own, low, vol, grad, sems):
    copies = [
        pltpu.make_async_copy(source, target, sems.at[k])
        for k, (source, target) in enumerate(((vol_hbm, vol), (grad_hbm, grad)))
    ]
    for copy in copies:
        copy.start()
    for a, ref in enumerate((vol, grad)):
        copies[a].wait()
        for x in range(8):
            tile = ref[0, x].reshape(T, 16).astype(F32).T.astype(BF)
            own[a, x] = tile
            if x < 4:
                low[a, x] = tile


def weight_kernel(w1_hbm, w2_hbm, out, w1, w2, sems):
    copies = [
        pltpu.make_async_copy(source, target, sems.at[k])
        for k, (source, target) in enumerate(((w1_hbm, w1), (w2_hbm, w2)))
    ]
    for copy in copies:
        copy.start()
    for f, ref in enumerate((w1, w2)):
        copies[f].wait()
        for m in range(4):
            tiles = [ref[8 * m + u].astype(F32) if 8 * m + u < 27 else jnp.zeros((16, T), F32) for u in range(8)]
            for j, tile in enumerate(regroup(tiles)):
                out[j, 4 * f + m] = tile.astype(BF)


def gathered(ref, k):
    return ref[:, k].reshape(T, T)


def row_of(own, nextx, a, r):
    return (own[a, r] if r < 8 else nextx[a, r - 8]).astype(F32)


def edge_kernel(own, nextx, out):
    first = lanes() < 64
    for a in range(2):
        for p in range(6):
            odd = rolled(row_of(own, nextx, a, 2 * p + 1), 64)
            out[a, p] = jnp.where(first, row_of(own, nextx, a, 2 * p), odd).astype(BF)


def send_kernel(own, nextx, nexty, weights, send):
    for j in range(8):
        for a in range(2):
            for k in range(18):
                send[j, 18 * a + k] = own[a, k] if k < 8 else nextx[a, k - 8] if k < 12 else nexty[a, k - 12]
        for k in range(8):
            send[j, 36 + k] = weights[j, k]


def product(left, right, out, width):
    for n in range(0, width, 640):
        size = min(640, width - n)
        out[:, n : n + size] = jnp.dot(left, right[:, n : n + size], preferred_element_type=F32)


def cells(width):
    lane = lax.broadcasted_iota(jnp.int32, (16, width), 1)
    return lane % 256 // 16, lane % 16


def stacked(place, ref, first, count, r, side, value):
    for b in range(3):
        out_row = r - b + 1
        if not first <= out_row < first + count:
            continue
        if (b, out_row) in ((2, 7), (0, 8)):
            tile = (value.astype(F32) * jnp.where(place[0] == 7, 0.0, 1.0)).astype(BF)
        else:
            tile = value
        at = (2 * (out_row - first) + side) * T
        ref[b * T : b * T + T, at : at + T] = tile


def combine(prods, sign, width, place):
    column, depth = cells(width)
    split_y = place[1] == 7
    apart = {1: (column == 7) & split_y, -1: (column == 8) & split_y}
    total = None
    for e in range(3):
        part = None
        for c in range(3):
            k = (3 * c + e) * 16
            term = prods[k : k + 16, :]
            step = sign * (c - 1)
            if step:
                term = jnp.where(apart[step], 0.0, rolled(term, -step * 16))
            part = term if part is None else part + term
        step = sign * (e - 1)
        if step:
            part = rolled(part, -step)
            part = jnp.where(depth != (15 if step > 0 else 0), part, 0.0)
        total = part if total is None else total + part
    return total


def shifted(field, place, out):
    column, depth = cells(OWN)
    split_y = place[1] == 7
    for c in range(3):
        moved = rolled(field, (c - 1) * 16)
        if c != 1:
            moved = jnp.where((column == (8 if c == 2 else 7)) & split_y, 0.0, moved)
        for e in range(3):
            piece = rolled(moved, e - 1)
            if e != 1:
                piece = jnp.where(depth != (0 if e == 2 else 15), piece, 0.0)
            k = (c * 3 + e) * 16
            out[k : k + 16, :] = piece.astype(BF)


def correlate(shifts, field, out):
    total = lax.dot_general(shifts[...], field, (((1,), (1,)), ((), ())), preferred_element_type=F32)
    for a in range(3):
        out[a * 144 : a * 144 + 144, :] = total[:, a * T : a * T + T]


def by_tap(filters, sign):
    parts = [filters[a * 144 : a * 144 + 144] for a in range(3)]
    return jnp.concatenate(parts[::sign], axis=1)


def gathered_filter(ref, first):
    parts = [gathered(ref, first + m).astype(F32).T.astype(BF) for m in range(4)]
    return jnp.concatenate(parts, axis=0)[0:432]


def first_kernel(place, block, w1rows, send, sums, vol, grad, prods1, prods2, shifts):
    for a, ref in enumerate((vol, grad)):
        for r in range(12):
            value = gathered(block, 18 * a + 12 + r // 2)
            value = rolled(value.astype(F32), 64).astype(BF) if r % 2 else value
            stacked(place, ref, 1, 10, r, 0, gathered(block, 18 * a + r))
            stacked(place, ref, 1, 10, r, 1, value)
    product(by_tap(w1rows[...].reshape(432, T), 1), vol, prods1, MID)
    product(by_tap(gathered_filter(block, 40), -1), grad, prods2, MID)

    pre = combine(prods1, 1, MID, place).astype(BF).astype(F32)
    sig = jax.nn.sigmoid(pre)
    hidden = (pre * sig).astype(BF).astype(F32)
    back = combine(prods2, -1, MID, place)
    back = (back * sig * (1.0 + pre * (1.0 - sig))).astype(BF).astype(F32)

    narrow = lanes()
    for a, field in enumerate((hidden, back)):
        packed = [None] * 3
        for r in range(10):
            inner = field[:, 2 * r * T : (2 * r + 1) * T]
            outer = field[:, (2 * r + 1) * T : (2 * r + 2) * T]
            tile_r = jnp.where(narrow < 16, rolled(outer, -32), inner).astype(BF)
            q, k = r // 4, r % 4
            moved = rolled(outer, 32 * k)
            packed[q] = moved if packed[q] is None else jnp.where(narrow // 32 == k, moved, packed[q])
            for j in range(8):
                send[j, a * 13 + r] = tile_r
        for q in range(3):
            tile_q = packed[q].astype(BF)
            for j in range(8):
                send[j, a * 13 + 10 + q] = tile_q

    column, _ = cells(OWN)
    inside = (column >= 2) & (column < 10)
    shifted(jnp.where(inside, back[:, 2 * T : 2 * T + OWN], 0.0), place, shifts)
    correlate(shifts, vol[:, 2 * T : 2 * T + OWN], sums)


def spread(place, middle, a, ref):
    lane = lanes(T)
    for r in range(10):
        inner = gathered(middle, a * 13 + r)
        outer = rolled(gathered(middle, a * 13 + 10 + r // 4).astype(F32), -32 * (r % 4))
        outer = jnp.where(lane < 32, outer, rolled(inner.astype(F32), 32)).astype(BF)
        stacked(place, ref, 2, 8, r + 1, 0, inner)
        stacked(place, ref, 2, 8, r + 1, 1, outer)


def grad_kernel(place, own, nextx, nexty, middle, sums1, send, hid, field, shifts, sums2):
    spread(place, middle, 0, hid)
    lane = lanes()
    for r in range(2, 10):
        field[:, (2 * r - 4) * T : (2 * r - 3) * T] = jnp.where(lane >= 32, row_of(own, nextx, 1, r), 0.0)
        tile = nexty[1, r // 2].astype(F32)
        tile = rolled(tile, 64) if r % 2 else tile
        field[:, (2 * r - 3) * T : (2 * r - 2) * T] = jnp.where(lane < 32, tile, 0.0)
    shifted(field[...], place, shifts)
    correlate(shifts, hid[...], sums2)
    rows = jnp.concatenate([sums1[...], sums2[...], jnp.zeros((32, T), F32)], axis=0)
    send[...] = rows.astype(BF).reshape(8, 112, T)


def second_kernel(place, block, middle, w2rows, keep, give, hid, pre, prods):
    spread(place, middle, 0, hid)
    spread(place, middle, 1, pre)

    def store(which, value):
        for x in range(8):
            for side in range(2):
                tile = value[:, (2 * x + side) * T : (2 * x + side + 1) * T].astype(BF)
                if x < 6:
                    keep[which, x, side] = tile
                else:
                    give[which, x - 6, side] = tile

    product(by_tap(w2rows[...].reshape(432, T), 1), hid, prods, OWN)
    store(0, combine(prods, 1, OWN, place))
    product(by_tap(gathered_filter(block, 36), -1), pre, prods, OWN)
    store(1, combine(prods, -1, OWN, place))


def back_kernel(keep, taken, rows, give):
    lane = lanes()
    for a in range(2):
        for q in range(2):
            packed = None
            for k in range(4):
                x = 4 * q + k
                tiles = taken.at[a, x] if x < 2 else keep.at[a, x - 2]
                rows[a, x] = tiles[0]
                moved = rolled(tiles[1].astype(F32), 32 * k)
                packed = moved if packed is None else jnp.where(lane // 32 == k, moved, packed)
            give[a, q] = packed.astype(BF)


def out_kernel(rows, taken, out, vgrad):
    lane = lanes()
    for a, ref in enumerate((out, vgrad)):
        for x in range(8):
            first = rolled(taken[a, x // 4].astype(F32), -32 * (x % 4))
            tile = jnp.where(lane < 32, first, rows[a, x].astype(F32))
            ref[0, x] = tile.T.astype(BF).reshape(8, 16, 16)


def sum_kernel(factor, parts, out):
    total = parts[0].astype(F32)
    for k in range(1, parts.shape[0]):
        total = total + parts[k].astype(F32)
    total = total * factor
    if out.shape == total.shape:
        out[...] = total
    else:
        for j in range(out.shape[0]):
            out[j] = total.astype(BF)


def last_kernel(parts, first, second):
    rows = parts[...].reshape(896, T).astype(F32)
    first[...] = rows[0:432].reshape(27, 16, T)
    second[...] = rows[432:864].reshape(27, 16, T)


def shape(*dims, dtype=BF):
    return jax.ShapeDtypeStruct(dims, dtype)


def cyclic(x, axis, step):
    size = lax.axis_size(axis)
    return lax.ppermute(x, axis, [(i, (i + step) % size) for i in range(size)])


def on_device(volume, first_filter, second_filter, out_grad):
    factor = 1.0 / math.sqrt(64 * 64 * 16)
    place = jnp.stack([lax.axis_index("gx"), lax.axis_index(GY)]).astype(jnp.int32)
    w1 = first_filter.transpose(1, 0, 2)
    w2 = second_filter.transpose(1, 0, 2)
    two = shape(2, 8, 16, T)
    own, low = call(
        pack_kernel,
        (two, shape(2, 4, 16, T)),
        [pltpu.VMEM((1, 8, 8, 16, 16), BF)] * 2 + [pltpu.SemaphoreType.DMA((2,))],
        hbm=True,
    )(volume, out_grad)
    nextx = cyclic(low, "gx", -1)
    pieces = call(
        weight_kernel,
        shape(8, 8, 16, T),
        [pltpu.VMEM((27, 16, T), BF)] * 2 + [pltpu.SemaphoreType.DMA((2,))],
        hbm=True,
    )(w1, w2)
    nextx, pieces = lax.optimization_barrier((nextx, pieces))
    nexty = cyclic(call(edge_kernel, shape(2, 6, 16, T))(own, nextx), GY, -1)
    nexty, place = lax.optimization_barrier((nexty, place))
    block = lax.all_to_all(call(send_kernel, shape(8, 44, 16, T))(own, nextx, nexty, pieces), "af", 0, 0)
    middle, sums = call(
        first_kernel,
        (shape(8, 26, 16, T), shape(432, T, dtype=F32)),
        [
            pltpu.VMEM((3 * T, MID), BF),
            pltpu.VMEM((3 * T, MID), BF),
            pltpu.VMEM((144, MID), F32),
            pltpu.VMEM((144, MID), F32),
            pltpu.VMEM((144, OWN), BF),
        ],
        scalars=True,
        limit=28,
    )(place, block, w1)
    middle = lax.all_to_all(middle, "af", 0, 0)
    many = shape(8, 112, T)
    parts = call(
        grad_kernel,
        many,
        [
            pltpu.VMEM((3 * T, OWN), BF),
            pltpu.VMEM((16, OWN), F32),
            pltpu.VMEM((144, OWN), BF),
            pltpu.VMEM((432, T), F32),
        ],
        scalars=True,
        limit=16,
    )(place, own, nextx, nexty, middle, sums)
    keep, give = call(
        second_kernel,
        (shape(2, 6, 2, 16, T), shape(2, 2, 2, 16, T)),
        [pltpu.VMEM((3 * T, OWN), BF)] * 2 + [pltpu.VMEM((144, OWN), F32)],
        scalars=True,
        limit=20,
    )(place, block, middle, w2)
    parts = lax.all_to_all(parts, "gx", 0, 0, axis_index_groups=[[0, 4, 1, 5, 2, 6, 3, 7]])
    parts, keep, give = lax.optimization_barrier((parts, keep, give))
    parts = call(functools.partial(sum_kernel, 1.0), many)(parts)
    rows, give = call(back_kernel, (two, shape(2, 2, 16, T)))(keep, cyclic(give, "gx", 1))
    parts = lax.all_to_all(parts, ("y0", "y1", "co"), 0, 0)
    parts, rows, give = lax.optimization_barrier((parts, rows, give))
    parts = call(functools.partial(sum_kernel, factor), many)(parts)
    output, volume_grad = call(out_kernel, (shape(1, 8, 8, 16, 16), shape(1, 8, 8, 16, 16)))(rows, cyclic(give, GY, 1))
    parts = lax.all_to_all(parts, "gx", 0, 0, axis_index_groups=[[0, 4, 1, 5, 2, 6, 3, 7]])
    wide = shape(27, 16, T, dtype=F32)
    first_grad, second_grad = call(last_kernel, (wide, wide))(parts)
    return output, volume_grad, first_grad.transpose(1, 0, 2), second_grad.transpose(1, 0, 2)


def solution(mesh):
    split = jax.sharding.Mesh(mesh.devices.reshape(8, 2, 2, 2, 8), ("gx", "y1", "y0", "co", "af"))
    cells = P(None, "gx", GY, None, "af")
    weights = P("af", None, None)
    return jax.shard_map(
        on_device,
        mesh=split,
        in_specs=(cells, weights, weights, cells),
        out_specs=(cells, cells, weights, weights),
        check_vma=False,
    )
```

```python
import functools
import math

import jax
import jax.numpy as jnp
from jax import lax
from jax.experimental import pallas as pl
from jax.experimental.pallas import tpu as pltpu
from jax.sharding import PartitionSpec as P

BF = jnp.bfloat16
F32 = jnp.float32
T = 128
VMEM = pl.BlockSpec(memory_space=pltpu.VMEM)
SMEM = pl.BlockSpec(memory_space=pltpu.SMEM)
HBM = pl.BlockSpec(memory_space=pltpu.HBM)
GY = ("y1", "y0", "co")
MID = 20 * T
OWN = 16 * T


def call(kernel, outs, scratch=(), scalars=False, hbm=False, limit=8):
    def run(*args):
        return pl.pallas_call(
            kernel,
            out_shape=outs,
            in_specs=[HBM if hbm else SMEM if scalars and k == 0 else VMEM for k in range(len(args))],
            scratch_shapes=scratch,
            compiler_params=pltpu.CompilerParams(vmem_limit_bytes=limit << 20),
        )(*args)

    return run


def lanes(rows=16):
    return lax.broadcasted_iota(jnp.int32, (rows, T), 1)


def rolled(x, shift):
    size = x.shape[1]
    return pltpu.roll(x, shift % size, 1) if shift % size else x


def regroup(tiles):
    lane = lanes()
    tiles = list(tiles)
    for bit in (1, 2, 4):
        clear = (lane // (16 * bit)) % 2 == 0
        for u in range(8):
            if u & bit:
                continue
            first, second = tiles[u], tiles[u + bit]
            tiles[u] = jnp.where(clear, first, rolled(second, 16 * bit))
            tiles[u + bit] = jnp.where(clear, rolled(first, -16 * bit), second)
    return tiles


def pack_kernel(vol_hbm, grad_hbm, own, low, vol, grad, sems):
    copies = [
        pltpu.make_async_copy(source, target, sems.at[k])
        for k, (source, target) in enumerate(((vol_hbm, vol), (grad_hbm, grad)))
    ]
    for copy in copies:
        copy.start()
    for a, ref in enumerate((vol, grad)):
        copies[a].wait()
        for x in range(8):
            tile = ref[0, x].reshape(T, 16).astype(F32).T.astype(BF)
            own[a, x] = tile
            if x < 4:
                low[a, x] = tile


def weight_kernel(w1_hbm, w2_hbm, out, w1, w2, sems):
    copies = [
        pltpu.make_async_copy(source, target, sems.at[k])
        for k, (source, target) in enumerate(((w1_hbm, w1), (w2_hbm, w2)))
    ]
    for copy in copies:
        copy.start()
    for f, ref in enumerate((w1, w2)):
        copies[f].wait()
        for m in range(4):
            tiles = [ref[8 * m + u].astype(F32) if 8 * m + u < 27 else jnp.zeros((16, T), F32) for u in range(8)]
            for j, tile in enumerate(regroup(tiles)):
                out[j, 4 * f + m] = tile.astype(BF)


def gathered(ref, k):
    return ref[:, k].reshape(T, T)


def row_of(own, nextx, a, r):
    return (own[a, r] if r < 8 else nextx[a, r - 8]).astype(F32)


def edge_kernel(own, nextx, out):
    first = lanes() < 64
    for a in range(2):
        for p in range(6):
            odd = rolled(row_of(own, nextx, a, 2 * p + 1), 64)
            out[a, p] = jnp.where(first, row_of(own, nextx, a, 2 * p), odd).astype(BF)


def send_kernel(own, nextx, nexty, weights, send):
    for j in range(8):
        for a in range(2):
            for k in range(18):
                send[j, 18 * a + k] = own[a, k] if k < 8 else nextx[a, k - 8] if k < 12 else nexty[a, k - 12]
        for k in range(8):
            send[j, 36 + k] = weights[j, k]


def product(left, right, out, width):
    for n in range(0, width, 640):
        size = min(640, width - n)
        out[:, n : n + size] = jnp.dot(left, right[:, n : n + size], preferred_element_type=F32)


def cells(width):
    lane = lax.broadcasted_iota(jnp.int32, (16, width), 1)
    return lane % 256 // 16, lane % 16


def stacked(place, ref, first, count, r, side, value):
    for b in range(3):
        out_row = r - b + 1
        if not first <= out_row < first + count:
            continue
        if (b, out_row) in ((2, 7), (0, 8)):
            tile = (value.astype(F32) * jnp.where(place[0] == 7, 0.0, 1.0)).astype(BF)
        else:
            tile = value
        at = (2 * (out_row - first) + side) * T
        ref[b * T : b * T + T, at : at + T] = tile


def combine(prods, sign, width, place):
    column, depth = cells(width)
    split_y = place[1] == 7
    apart = {1: (column == 7) & split_y, -1: (column == 8) & split_y}
    total = None
    for e in range(3):
        part = None
        for c in range(3):
            k = (3 * c + e) * 16
            term = prods[k : k + 16, :]
            step = sign * (c - 1)
            if step:
                term = jnp.where(apart[step], 0.0, rolled(term, -step * 16))
            part = term if part is None else part + term
        step = sign * (e - 1)
        if step:
            part = rolled(part, -step)
            part = jnp.where(depth != (15 if step > 0 else 0), part, 0.0)
        total = part if total is None else total + part
    return total


def shifted(field, place, out):
    column, depth = cells(OWN)
    split_y = place[1] == 7
    for c in range(3):
        moved = rolled(field, (c - 1) * 16)
        if c != 1:
            moved = jnp.where((column == (8 if c == 2 else 7)) & split_y, 0.0, moved)
        for e in range(3):
            piece = rolled(moved, e - 1)
            if e != 1:
                piece = jnp.where(depth != (0 if e == 2 else 15), piece, 0.0)
            k = (c * 3 + e) * 16
            out[k : k + 16, :] = piece.astype(BF)


def correlate(shifts, field, out):
    total = lax.dot_general(shifts[...], field, (((1,), (1,)), ((), ())), preferred_element_type=F32)
    for a in range(3):
        out[a * 144 : a * 144 + 144, :] = total[:, a * T : a * T + T]


def by_tap(filters, sign):
    parts = [filters[a * 144 : a * 144 + 144] for a in range(3)]
    return jnp.concatenate(parts[::sign], axis=1)


def gathered_filter(ref, first):
    parts = [gathered(ref, first + m).astype(F32).T.astype(BF) for m in range(4)]
    return jnp.concatenate(parts, axis=0)[0:432]


def first_kernel(place, block, w1rows, send, sums, vol, grad, prods1, prods2, shifts):
    for a, ref in enumerate((vol, grad)):
        for r in range(12):
            value = gathered(block, 18 * a + 12 + r // 2)
            value = rolled(value.astype(F32), 64).astype(BF) if r % 2 else value
            stacked(place, ref, 1, 10, r, 0, gathered(block, 18 * a + r))
            stacked(place, ref, 1, 10, r, 1, value)
    product(by_tap(w1rows[...].reshape(432, T), 1), vol, prods1, MID)
    product(by_tap(gathered_filter(block, 40), -1), grad, prods2, MID)

    pre = combine(prods1, 1, MID, place).astype(BF).astype(F32)
    sig = jax.nn.sigmoid(pre)
    hidden = (pre * sig).astype(BF).astype(F32)
    back = combine(prods2, -1, MID, place)
    back = (back * sig * (1.0 + pre * (1.0 - sig))).astype(BF).astype(F32)

    narrow = lanes()
    for a, field in enumerate((hidden, back)):
        packed = [None] * 3
        for r in range(10):
            inner = field[:, 2 * r * T : (2 * r + 1) * T]
            outer = field[:, (2 * r + 1) * T : (2 * r + 2) * T]
            tile_r = jnp.where(narrow < 16, rolled(outer, -32), inner).astype(BF)
            q, k = r // 4, r % 4
            moved = rolled(outer, 32 * k)
            packed[q] = moved if packed[q] is None else jnp.where(narrow // 32 == k, moved, packed[q])
            for j in range(8):
                send[j, a * 13 + r] = tile_r
        for q in range(3):
            tile_q = packed[q].astype(BF)
            for j in range(8):
                send[j, a * 13 + 10 + q] = tile_q

    column, _ = cells(OWN)
    inside = (column >= 2) & (column < 10)
    shifted(jnp.where(inside, back[:, 2 * T : 2 * T + OWN], 0.0), place, shifts)
    correlate(shifts, vol[:, 2 * T : 2 * T + OWN], sums)


def spread(place, middle, a, ref):
    lane = lanes(T)
    for r in range(10):
        inner = gathered(middle, a * 13 + r)
        outer = rolled(gathered(middle, a * 13 + 10 + r // 4).astype(F32), -32 * (r % 4))
        outer = jnp.where(lane < 32, outer, rolled(inner.astype(F32), 32)).astype(BF)
        stacked(place, ref, 2, 8, r + 1, 0, inner)
        stacked(place, ref, 2, 8, r + 1, 1, outer)


def grad_kernel(place, own, nextx, nexty, middle, sums1, send, hid, field, shifts, sums2):
    spread(place, middle, 0, hid)
    lane = lanes()
    for r in range(2, 10):
        field[:, (2 * r - 4) * T : (2 * r - 3) * T] = jnp.where(lane >= 32, row_of(own, nextx, 1, r), 0.0)
        tile = nexty[1, r // 2].astype(F32)
        tile = rolled(tile, 64) if r % 2 else tile
        field[:, (2 * r - 3) * T : (2 * r - 2) * T] = jnp.where(lane < 32, tile, 0.0)
    shifted(field[...], place, shifts)
    correlate(shifts, hid[...], sums2)
    rows = jnp.concatenate([sums1[...], sums2[...], jnp.zeros((32, T), F32)], axis=0)
    send[...] = rows.astype(BF).reshape(8, 112, T)


def second_kernel(place, block, middle, w2rows, keep, give, hid, pre, prods):
    spread(place, middle, 0, hid)
    spread(place, middle, 1, pre)

    def store(which, value):
        for x in range(8):
            for side in range(2):
                tile = value[:, (2 * x + side) * T : (2 * x + side + 1) * T].astype(BF)
                if x < 6:
                    keep[which, x, side] = tile
                else:
                    give[which, x - 6, side] = tile

    product(by_tap(w2rows[...].reshape(432, T), 1), hid, prods, OWN)
    store(0, combine(prods, 1, OWN, place))
    product(by_tap(gathered_filter(block, 36), -1), pre, prods, OWN)
    store(1, combine(prods, -1, OWN, place))


def back_kernel(keep, taken, rows, give):
    lane = lanes()
    for a in range(2):
        for q in range(2):
            packed = None
            for k in range(4):
                x = 4 * q + k
                tiles = taken.at[a, x] if x < 2 else keep.at[a, x - 2]
                rows[a, x] = tiles[0]
                moved = rolled(tiles[1].astype(F32), 32 * k)
                packed = moved if packed is None else jnp.where(lane // 32 == k, moved, packed)
            give[a, q] = packed.astype(BF)


def out_kernel(rows, taken, out, vgrad):
    lane = lanes()
    for a, ref in enumerate((out, vgrad)):
        for x in range(8):
            first = rolled(taken[a, x // 4].astype(F32), -32 * (x % 4))
            tile = jnp.where(lane < 32, first, rows[a, x].astype(F32))
            ref[0, x] = tile.T.astype(BF).reshape(8, 16, 16)


def sum_kernel(factor, parts, out):
    total = parts[0].astype(F32)
    for k in range(1, parts.shape[0]):
        total = total + parts[k].astype(F32)
    total = total * factor
    if out.shape == total.shape:
        out[...] = total
    else:
        for j in range(out.shape[0]):
            out[j] = total.astype(BF)


def last_kernel(parts, first, second):
    rows = parts[...].reshape(896, T).astype(F32)
    first[...] = rows[0:432].reshape(27, 16, T)
    second[...] = rows[432:864].reshape(27, 16, T)


def shape(*dims, dtype=BF):
    return jax.ShapeDtypeStruct(dims, dtype)


def cyclic(x, axis, step):
    size = lax.axis_size(axis)
    return lax.ppermute(x, axis, [(i, (i + step) % size) for i in range(size)])


def on_device(volume, first_filter, second_filter, out_grad):
    factor = 1.0 / math.sqrt(64 * 64 * 16)
    place = jnp.stack([lax.axis_index("gx"), lax.axis_index(GY)]).astype(jnp.int32)
    w1 = first_filter.transpose(1, 0, 2)
    w2 = second_filter.transpose(1, 0, 2)
    two = shape(2, 8, 16, T)
    own, low = call(
        pack_kernel,
        (two, shape(2, 4, 16, T)),
        [pltpu.VMEM((1, 8, 8, 16, 16), BF)] * 2 + [pltpu.SemaphoreType.DMA((2,))],
        hbm=True,
    )(volume, out_grad)
    nextx = cyclic(low, "gx", -1)
    pieces = call(
        weight_kernel,
        shape(8, 8, 16, T),
        [pltpu.VMEM((27, 16, T), BF)] * 2 + [pltpu.SemaphoreType.DMA((2,))],
        hbm=True,
    )(w1, w2)
    nextx, pieces = lax.optimization_barrier((nextx, pieces))
    nexty = cyclic(call(edge_kernel, shape(2, 6, 16, T))(own, nextx), GY, -1)
    nexty, place = lax.optimization_barrier((nexty, place))
    block = lax.all_to_all(call(send_kernel, shape(8, 44, 16, T))(own, nextx, nexty, pieces), "af", 0, 0)
    middle, sums = call(
        first_kernel,
        (shape(8, 26, 16, T), shape(432, T, dtype=F32)),
        [
            pltpu.VMEM((3 * T, MID), BF),
            pltpu.VMEM((3 * T, MID), BF),
            pltpu.VMEM((144, MID), F32),
            pltpu.VMEM((144, MID), F32),
            pltpu.VMEM((144, OWN), BF),
        ],
        scalars=True,
        limit=28,
    )(place, block, w1)
    middle = lax.all_to_all(middle, "af", 0, 0)
    many = shape(8, 112, T)
    parts = call(
        grad_kernel,
        many,
        [
            pltpu.VMEM((3 * T, OWN), BF),
            pltpu.VMEM((16, OWN), F32),
            pltpu.VMEM((144, OWN), BF),
            pltpu.VMEM((432, T), F32),
        ],
        scalars=True,
        limit=16,
    )(place, own, nextx, nexty, middle, sums)
    keep, give = call(
        second_kernel,
        (shape(2, 6, 2, 16, T), shape(2, 2, 2, 16, T)),
        [pltpu.VMEM((3 * T, OWN), BF)] * 2 + [pltpu.VMEM((144, OWN), F32)],
        scalars=True,
        limit=20,
    )(place, block, middle, w2)
    parts = lax.all_to_all(parts, "gx", 0, 0, axis_index_groups=[[0, 4, 1, 5, 2, 6, 3, 7]])
    parts, keep, give = lax.optimization_barrier((parts, keep, give))
    parts = call(functools.partial(sum_kernel, 1.0), many)(parts)
    rows, give = call(back_kernel, (two, shape(2, 2, 16, T)))(keep, cyclic(give, "gx", 1))
    parts = lax.all_to_all(parts, ("y0", "co", "y1"), 0, 0)
    parts, rows, give = lax.optimization_barrier((parts, rows, give))
    parts = call(functools.partial(sum_kernel, factor), many)(parts)
    output, volume_grad = call(out_kernel, (shape(1, 8, 8, 16, 16), shape(1, 8, 8, 16, 16)))(rows, cyclic(give, GY, 1))
    parts = lax.all_to_all(parts, "gx", 0, 0, axis_index_groups=[[0, 4, 1, 5, 2, 6, 3, 7]])
    wide = shape(27, 16, T, dtype=F32)
    first_grad, second_grad = call(last_kernel, (wide, wide))(parts)
    return output, volume_grad, first_grad.transpose(1, 0, 2), second_grad.transpose(1, 0, 2)


def solution(mesh):
    split = jax.sharding.Mesh(mesh.devices.reshape(8, 2, 2, 2, 8), ("gx", "y1", "y0", "co", "af"))
    cells = P(None, "gx", GY, None, "af")
    weights = P("af", None, None)
    return jax.shard_map(
        on_device,
        mesh=split,
        in_specs=(cells, weights, weights, cells),
        out_specs=(cells, cells, weights, weights),
        check_vma=False,
    )
```
